32 devices in a mesh: ctx: 16 (over z, y, x), ch: 2 (over core).
Axes of the slice: x: 2, y: 2, z: 4, core: 2. Of those that a mesh axis runs over, the one named last changes fastest.
Arguments:
- conv_input: bfloat16 [2048, 4096], P('ctx', 'ch'), may hold values from -6 to 6
- residues: float32 [4096, 16], P('ch'), may hold values from -4 to 4
- decay_rates: float32 [4096, 16], P('ch'), as said below
- skip_gain: float32 [4096], P('ch'), may hold values from -1 to 1
- query_rows: bfloat16 [2048, 4096], P('ctx', 'ch'), may hold values from -5 to 5
- key_rows: bfloat16 [2048, 4096], P('ctx', 'ch'), may hold values from -5 to 5
- value_rows: bfloat16 [2048, 4096], P('ctx', 'ch'), may hold values from -16 to 16
- norm_gain: float32 [4096], P('ch'), may hold values from 0.5 to 1.5
Outputs:
- conv_out: bfloat16 [2048, 4096], P('ctx', 'ch')
- attended: bfloat16 [2048, 4096], P('ctx', 'ch')
The draws below stay inside these ranges and needn't reach their ends.
Inputs may be any that keep to these rules, and one draw needn't show every extreme that they name: `decay_rates`: decay rates lie between 0.5 / 2048 and 1 / 30.
All inputs are finite; a program needn't handle non-finite values.
Results may differ from the reference program's by a relative error of at most 0.019.
Values may be sent and summed in bfloat16 or wider, within the bound.
A program may use at most 64 MiB of HBM per device.

```python
import math
import jax
import jax.numpy as jnp
from jax import lax

HEADS = 32
HD = 128
MODES = 16
TOK_DEV = 128
SEQ = 2048
WIDTH = 4096
CH = 4096
N_CTX = 16


def draw_decay_rates(key, part):
    lowest = math.log(0.5 / SEQ)
    highest = math.log(1.0 / 30.0)
    unit_draw = jax.random.uniform(key, (CH, MODES), jnp.float32)
    return jnp.exp(lowest + (highest - lowest) * unit_draw)


def attention_tables(key):
    query_seed = jax.random.fold_in(key, 101)
    key_seed = jax.random.fold_in(key, 202)
    table_shape = (SEQ, HEADS * HD)
    query_table = jnp.clip(jax.random.normal(query_seed, table_shape, jnp.float32), -5.0, 5.0)
    key_table = jnp.clip(jax.random.normal(key_seed, table_shape, jnp.float32), -5.0, 5.0)
    return (query_table, key_table)


def draw_query_rows(key, part):
    return attention_tables(key)[0].astype(jnp.bfloat16)


def draw_key_rows(key, part):
    return attention_tables(key)[1].astype(jnp.bfloat16)


def draw_value_rows(key, part):
    table_shape = (SEQ, HEADS * HD)
    column = jnp.arange(HEADS * HD, dtype=jnp.float32) / (HEADS * HD - 1)
    base_seed = jax.random.fold_in(key, 404)
    base_table = jnp.clip(jax.random.normal(base_seed, table_shape, jnp.float32), -5.0, 5.0)
    growth = jnp.exp(math.log(3.0) * column)
    return (base_table * growth[None, :]).astype(jnp.bfloat16)


def block_levels(key, extent, shards, smallest, largest):
    def one(axis_at, blocks):
        heights = jax.random.uniform(jax.random.fold_in(jax.random.fold_in(key, 6), axis_at), (blocks,), jnp.float32, smallest / len(shards), largest / len(shards))
        return jnp.repeat(jnp.exp(heights), extent[axis_at] // blocks).reshape((-1,) + (1,) * (len(extent) - axis_at - 1))

    gain = one(*shards[0])
    for cut in shards[1:]:
        gain = gain * one(*cut)
    return gain


def noise(own_key, dims, deviation, limit, cuts=(), held_as=jnp.bfloat16):
    loudness = block_levels(own_key, dims, cuts, -0.22, 0.18) if cuts else 1.0
    values = jax.random.normal(own_key, dims, jnp.float32) * deviation * loudness
    return jnp.minimum(jnp.maximum(values, -limit), limit).astype(held_as)


def setup_inputs(seed: int = 0) -> dict:
    key_of = jax.random.split(jax.random.key(seed), 9)
    return {
        "conv_input": noise(key_of[0], (SEQ, CH), 1.0, 6.0, ((0, 16), (1, 2))),
        "residues": noise(key_of[1], (CH, MODES), 0.25, 4.0, ((0, 2),), jnp.float32),
        "decay_rates": draw_decay_rates(jax.random.fold_in(key_of[8], 71), 0),
        "skip_gain": jnp.clip(jax.random.uniform(key_of[3], (CH,), jnp.float32, -1.0, 1.0) * block_levels(key_of[3], (CH,), ((0, 2),), -0.4, 0.0), -1.0, 1.0),
        "query_rows": draw_query_rows(jax.random.fold_in(key_of[8], 71), 0),
        "key_rows": draw_key_rows(jax.random.fold_in(key_of[8], 71), 0),
        "value_rows": draw_value_rows(jax.random.fold_in(key_of[8], 71), 0),
        "norm_gain": jnp.clip(1.0 + 0.1 * jax.random.normal(key_of[7], (WIDTH,), jnp.float32), 0.5, 1.5),
    }


def attend_block(block_index, query_rows, key_padded, value_padded):
    start_row = block_index * TOK_DEV
    query_block = lax.dynamic_slice_in_dim(query_rows, start_row, TOK_DEV, 0).astype(jnp.float32).reshape(TOK_DEV, HEADS, HD)
    key_block = lax.dynamic_slice_in_dim(key_padded, start_row, 2 * TOK_DEV, 0).astype(jnp.float32).reshape(2 * TOK_DEV, HEADS, HD)
    value_block = lax.dynamic_slice_in_dim(value_padded, start_row, 2 * TOK_DEV, 0).astype(jnp.float32).reshape(2 * TOK_DEV, HEADS, HD)
    scores = jnp.einsum('qhd,khd->hqk', query_block, key_block) * HD ** (-0.5)
    query_place = jnp.arange(TOK_DEV, dtype=jnp.int32)[:, None]
    key_place = jnp.arange(2 * TOK_DEV, dtype=jnp.int32)[None, :] - TOK_DEV
    allowed = (key_place <= query_place) & ((key_place >= 0) | (block_index > 0))
    scores = jnp.where(allowed[None], scores, -jnp.inf)
    row_max = lax.optimization_barrier(jnp.max(scores, axis=-1, keepdims=True))
    weights = jnp.exp(scores - row_max)
    row_total = lax.optimization_barrier(jnp.sum(weights, axis=-1))
    rounded = weights.astype(jnp.bfloat16).astype(jnp.float32)
    mixed_heads = jnp.einsum('hqk,khd->qhd', rounded, value_block)
    mixed_heads = mixed_heads / jnp.transpose(row_total)[:, :, None]
    return mixed_heads.reshape(TOK_DEV, WIDTH).astype(jnp.bfloat16)

def reference(conv_input, residues, decay_rates, skip_gain, query_rows, key_rows, value_rows, norm_gain):
    signal = conv_input.astype(jnp.float32)
    step_axis = jnp.arange(SEQ, dtype=jnp.float32)[:, None]
    kernel = jnp.zeros((SEQ, CH), jnp.float32)
    for mode_index in range(MODES):
        decay_rate = decay_rates[:, mode_index]
        weight = residues[:, mode_index] * jnp.sqrt(-jnp.expm1(-decay_rate) * (1.0 + jnp.exp(-decay_rate)))
        kernel = kernel + weight[None, :] * jnp.exp(-decay_rate[None, :] * step_axis)
    spectrum = jnp.fft.rfft(signal, n=2 * SEQ, axis=0) * jnp.fft.rfft(kernel, n=2 * SEQ, axis=0)
    convolved = jnp.fft.irfft(spectrum, n=2 * SEQ, axis=0)[:SEQ]
    conv_out = (convolved + skip_gain[None, :] * signal).astype(jnp.bfloat16)
    gated = (value_rows.astype(jnp.float32) * conv_out.astype(jnp.float32)).astype(jnp.bfloat16)
    zero_block = jnp.zeros((TOK_DEV, WIDTH), jnp.bfloat16)
    key_padded = jnp.concatenate([zero_block, key_rows], axis=0)
    value_padded = jnp.concatenate([zero_block, gated], axis=0)
    blocks = lax.map(lambda block_index: attend_block(block_index, query_rows, key_padded, value_padded), jnp.arange(N_CTX, dtype=jnp.int32))
    attention = blocks.reshape(SEQ, WIDTH)
    attention_wide = attention.astype(jnp.float32)
    mean_square = lax.optimization_barrier(jnp.mean(attention_wide * attention_wide, axis=1))
    attended = (attention_wide * norm_gain[None, :] / jnp.sqrt(mean_square + 1e-06)[:, None]).astype(jnp.bfloat16)
    return (conv_out, attended)
```

```python
import functools
import math

import jax
import jax.numpy as jnp
import numpy as np
from jax import lax
from jax.experimental import pallas as pl
from jax.experimental.pallas import tpu as pltpu
from jax.sharding import PartitionSpec as P

HD = 128
LANES = 128
GROUP = 8
HEADS_PER_CHUNK = 4
MESH = pl.DeviceIdType.MESH


def scan_stages(count):
    stages = []
    stride = 1
    while stride < count:
        radix = 4 if count // stride >= 4 else 2
        stages.append((stride, radix))
        stride *= radix
    return stages


def split_bf16(value):
    high = value.astype(jnp.bfloat16)
    low = (value - high.astype(jnp.float32)).astype(jnp.bfloat16)
    return high, low


def dft_tables(rows):
    freq = 2 * np.arange(rows, dtype=np.int64)[:, None] + 1
    place = np.arange(rows, dtype=np.int64)[None, :]
    angle = (freq * place % (4 * rows)).astype(np.float64) * (math.pi / (2 * rows))
    forward = np.concatenate([np.cos(angle), -np.sin(angle)], axis=0)
    inverse = forward.T / rows
    parts = []
    for table in (forward, inverse):
        high = table.astype(jnp.bfloat16)
        low = (table - high.astype(np.float64)).astype(jnp.bfloat16)
        parts.append((high, low))
    (f_high, f_low), (i_high, i_low) = parts
    return (
        np.concatenate([f_high, f_low], axis=1),
        np.concatenate([f_high, f_high, f_low], axis=1),
        np.concatenate([i_high, i_high, i_low], axis=1),
    )


def kernel(
    ctx_count,
    ch_count,
    x_ref,
    rate_ref,
    res_ref,
    skip_ref,
    q_ref,
    k_ref,
    v_ref,
    gain_ref,
    fx_ref,
    fk_ref,
    inv_ref,
    conv_ref,
    out_ref,
    weight_s,
    taps_s,
    intra_s,
    state_s,
    enter_s,
    send_s,
    recv_s,
    gated_s,
    prev_k,
    prev_g,
    soft_s,
    own_s,
    norm_s,
    att_s,
    energy_s,
    energy_r,
    k_sem,
    g_send,
    g_recv,
    s_send,
    s_recv,
    e_send,
    e_recv,
):
    rows, chans = x_ref.shape
    modes = rate_ref.shape[0]
    tiles = chans // LANES
    groups = rows // GROUP
    heads = chans // HD
    chunks = heads // HEADS_PER_CHUNK
    chunk_cols = HEADS_PER_CHUNK * HD
    pos = lax.axis_index("ctx")
    core = lax.axis_index("ch")
    stages = scan_stages(ctx_count)

    offsets = {1}
    for stride, radix in stages:
        offsets |= {stride * m for m in range(1, radix)}
    offsets = sorted({o % ctx_count for o in offsets} | {-o % ctx_count for o in offsets})
    barrier = pltpu.get_barrier_semaphore()
    for o in offsets:
        pl.semaphore_signal(
            barrier, inc=1, device_id={"ctx": lax.rem(pos + o, ctx_count)}, device_id_type=MESH
        )
    for o in range(1, ch_count):
        pl.semaphore_signal(
            barrier, inc=1, device_id={"ch": lax.rem(core + o, ch_count)}, device_id_type=MESH
        )
    pl.semaphore_wait(barrier, len(offsets) + ch_count - 1)

    after = {"ctx": lax.rem(pos + 1, ctx_count)}
    has_after = pos + 1 < ctx_count
    has_before = pos > 0

    def key_copy():
        return pltpu.make_async_remote_copy(
            k_ref, prev_k, k_sem.at[0], k_sem.at[1], device_id=after, device_id_type=MESH
        )

    def gated_copy(c):
        part = pl.ds(c * chunk_cols, chunk_cols)
        return pltpu.make_async_remote_copy(
            gated_s.at[:, part],
            prev_g.at[:, part],
            g_send.at[c],
            g_recv.at[c],
            device_id=after,
            device_id_type=MESH,
        )

    def state_copy(level, slot, offset):
        return pltpu.make_async_remote_copy(
            send_s.at[level],
            recv_s.at[slot],
            s_send.at[slot],
            s_recv.at[slot],
            device_id={"ctx": lax.rem(pos + offset, ctx_count)},
            device_id_type=MESH,
        )

    @pl.when(has_after)
    def _():
        key_copy().start()

    @pl.when(jnp.logical_not(has_before))
    def _():
        prev_k[...] = jnp.zeros_like(prev_k)
        prev_g[...] = jnp.zeros_like(prev_g)

    u_place = lax.broadcasted_iota(jnp.int32, (1, GROUP, LANES), 1).astype(jnp.float32)

    def state_tile(j, carry):
        cols = pl.ds(pl.multiple_of(j * LANES, LANES), LANES)
        rate = rate_ref[:, cols]
        shrink = jnp.exp(-rate)
        weight_s[:, cols] = res_ref[:, cols] * jnp.sqrt((1.0 - shrink) * (1.0 + shrink))
        rate3 = rate[:, None, :]
        step = jnp.broadcast_to(jnp.exp(-GROUP * rate)[:, None, :], (modes, GROUP, LANES))
        x = x_ref[:, cols].astype(jnp.float32)
        total = jnp.broadcast_to(x[None, 0:GROUP], (modes, GROUP, LANES))
        for i in range(1, groups):
            total = total * step + x[None, i * GROUP : (i + 1) * GROUP]
        total = total * jnp.exp(-rate3 * (GROUP - 1.0 - u_place))
        state = jnp.sum(total, axis=1)
        state_s[:, cols] = state
        send_s[0, :, cols] = state.astype(jnp.bfloat16)
        return carry

    lax.fori_loop(0, tiles, state_tile, 0)

    def start_stage(level, base):
        stride, radix = stages[level]
        for m in range(1, radix):

            @pl.when(pos + m * stride < ctx_count)
            def _(m=m):
                state_copy(level, base + m - 1, m * stride).start()

            @pl.when(pos < m * stride)
            def _(m=m):
                recv_s[base + m - 1] = jnp.zeros(recv_s.shape[1:], recv_s.dtype)

    def wait_stage(level, base):
        stride, radix = stages[level]
        for m in range(1, radix):

            @pl.when(pos >= m * stride)
            def _(m=m):
                state_copy(level, base + m - 1, m * stride).wait_recv()

    def spread(cols, start):
        rate = rate_ref[:, cols]
        step = jnp.broadcast_to(jnp.exp(-GROUP * rate)[:, None, :], (modes, GROUP, LANES))
        term = start[:, None, :] * jnp.exp(-rate[:, None, :] * u_place)
        parts = []
        for i in range(groups):
            parts.append(jnp.sum(term, axis=0))
            if i + 1 < groups:
                term = term * step
        return jnp.concatenate(parts, axis=0)

    start_stage(0, 0)

    def taps_tile(j, carry):
        cols = pl.ds(pl.multiple_of(j * LANES, LANES), LANES)
        high, low = split_bf16(spread(cols, weight_s[:, cols]))
        taps_s[0:rows, cols] = high
        taps_s[rows : 2 * rows, cols] = low
        return carry

    lax.fori_loop(0, tiles, taps_tile, 0)

    wide = 2 * LANES

    def transform_tile(j, carry):
        cols = pl.ds(pl.multiple_of(j * wide, wide), wide)
        x = x_ref[:, cols]
        taps_high = taps_s[0:rows, cols]
        taps_low = taps_s[rows : 2 * rows, cols]
        spec = jnp.dot(
            fx_ref[...], jnp.concatenate([x, x], axis=0), preferred_element_type=jnp.float32
        )
        filt = jnp.dot(
            fk_ref[...],
            jnp.concatenate([taps_high, taps_low, taps_high], axis=0),
            preferred_element_type=jnp.float32,
        )
        s_re, s_im = spec[:rows], spec[rows:]
        f_re, f_im = filt[:rows], filt[rows:]
        product = jnp.concatenate([s_re * f_re - s_im * f_im, s_re * f_im + s_im * f_re], axis=0)
        high, low = split_bf16(product)
        intra_s[:, cols] = jnp.dot(
            inv_ref[...],
            jnp.concatenate([high, low, high], axis=0),
            preferred_element_type=jnp.float32,
        )
        return carry

    lax.fori_loop(0, chans // wide, transform_tile, 0)

    base = 0
    for level, (stride, radix) in enumerate(stages):
        wait_stage(level, base)
        last = level + 1 == len(stages)

        def combine_tile(j, carry, level=level, stride=stride, radix=radix, base=base, last=last):
            cols = pl.ds(pl.multiple_of(j * LANES, LANES), LANES)
            rate = rate_ref[:, cols] * float(rows)
            entered = jnp.zeros((modes, LANES), jnp.float32)
            total = state_s[:, cols]
            for m in range(1, radix):
                got = recv_s[base + m - 1, :, cols].astype(jnp.float32)
                entered = entered + jnp.exp(-rate * (m * stride - 1.0)) * got
                if not last:
                    total = total + jnp.exp(-rate * (1.0 * m * stride)) * got
            if level > 0:
                entered = entered + enter_s[:, cols]
            enter_s[:, cols] = entered
            if not last:
                state_s[:, cols] = total
                send_s[level + 1, :, cols] = total.astype(jnp.bfloat16)
            return carry

        lax.fori_loop(0, tiles, combine_tile, 0)
        base += radix - 1
        if not last:
            start_stage(level + 1, base)

    def gated_tile(j, carry):
        cols = pl.ds(pl.multiple_of(j * LANES, LANES), LANES)
        start = weight_s[:, cols] * enter_s[:, cols] * jnp.exp(-rate_ref[:, cols])
        x = x_ref[:, cols].astype(jnp.float32)
        conv = intra_s[:, cols] + spread(cols, start) + skip_ref[:, cols] * x
        conv = conv.astype(jnp.bfloat16)
        conv_ref[:, cols] = conv
        gated = v_ref[:, cols].astype(jnp.float32) * conv.astype(jnp.float32)
        gated_s[:, cols] = gated.astype(jnp.bfloat16)
        return carry

    for c in range(chunks):
        lax.fori_loop(c * HEADS_PER_CHUNK, (c + 1) * HEADS_PER_CHUNK, gated_tile, 0)

        @pl.when(has_after)
        def _(c=c):
            gated_copy(c).start()

    @pl.when(has_before)
    def _():
        key_copy().wait_recv()

    q_place = lax.broadcasted_iota(jnp.int32, (rows, rows), 0)
    k_place = lax.broadcasted_iota(jnp.int32, (rows, rows), 1)
    causal = k_place <= q_place
    before_bias = jnp.where(has_before, 0.0, -jnp.inf)
    contract = (((1,), (1,)), ((), ()))

    def weight_head(h, carry):
        cols = pl.ds(pl.multiple_of(h * HD, HD), HD)
        q = q_ref[:, cols]
        scale = HD ** (-0.5)
        old = lax.dot_general(q, prev_k[:, cols], contract, preferred_element_type=jnp.float32)
        new = lax.dot_general(q, k_ref[:, cols], contract, preferred_element_type=jnp.float32)
        old = old * scale + before_bias
        new = jnp.where(causal, new * scale, -jnp.inf)
        top = jnp.max(jnp.maximum(old, new), axis=1, keepdims=True)
        old = jnp.exp(old - top)
        new = jnp.exp(new - top)
        total = jnp.sum(old + new, axis=1, keepdims=True)
        soft_s[:, cols] = old.astype(jnp.bfloat16)
        own_s[:, cols] = jnp.dot(
            new.astype(jnp.bfloat16), gated_s[:, cols], preferred_element_type=jnp.float32
        )
        norm_s[:, cols] = jnp.broadcast_to(1.0 / total, (rows, HD))
        return carry

    lax.fori_loop(0, heads, weight_head, 0)

    energy_s[...] = jnp.zeros_like(energy_s)

    def mix_head(h, carry):
        cols = pl.ds(pl.multiple_of(h * HD, HD), HD)
        mixed = own_s[:, cols] + jnp.dot(
            soft_s[:, cols], prev_g[:, cols], preferred_element_type=jnp.float32
        )
        attention = (mixed * norm_s[:, cols]).astype(jnp.bfloat16)
        att_s[:, cols] = attention
        attention = attention.astype(jnp.float32)
        energy_s[...] += attention * attention
        return carry

    for c in range(chunks):

        @pl.when(has_before)
        def _(c=c):
            gated_copy(c).wait_recv()

        lax.fori_loop(c * HEADS_PER_CHUNK, (c + 1) * HEADS_PER_CHUNK, mix_head, 0)

    def energy_copy(o):
        return pltpu.make_async_remote_copy(
            energy_s,
            energy_r.at[o - 1],
            e_send.at[o - 1],
            e_recv.at[o - 1],
            device_id={"ch": lax.rem(core + o, ch_count)},
            device_id_type=MESH,
        )

    for o in range(1, ch_count):
        energy_copy(o).start()
    energy = energy_s[...]
    for o in range(1, ch_count):
        energy_copy(o).wait_recv()
        energy = energy + energy_r[o - 1]
    mean_square = jnp.sum(energy, axis=1, keepdims=True) / float(chans * ch_count)
    factor = jnp.broadcast_to(lax.rsqrt(mean_square + 1e-6), (rows, LANES))

    def norm_tile(j, carry):
        cols = pl.ds(pl.multiple_of(j * LANES, LANES), LANES)
        attention = att_s[:, cols].astype(jnp.float32)
        out_ref[:, cols] = (attention * gain_ref[:, cols] * factor).astype(jnp.bfloat16)
        return carry

    lax.fori_loop(0, tiles, norm_tile, 0)

    for o in range(1, ch_count):
        energy_copy(o).wait_send()

    @pl.when(has_after)
    def _():
        key_copy().wait_send()
        for c in range(chunks):
            gated_copy(c).wait_send()

    base = 0
    for level, (stride, radix) in enumerate(stages):
        for m in range(1, radix):

            @pl.when(pos + m * stride < ctx_count)
            def _(level=level, slot=base + m - 1, offset=m * stride):
                state_copy(level, slot, offset).wait_send()

        base += radix - 1


def per_device(
    conv_input, residues, decay_rates, skip_gain, query_rows, key_rows, value_rows, norm_gain
):
    ctx_count = lax.axis_size("ctx")
    ch_count = lax.axis_size("ch")
    rows, chans = conv_input.shape
    modes = residues.shape[1]
    chunks = chans // (HEADS_PER_CHUNK * HD)
    stages = scan_stages(ctx_count)
    slots = sum(radix - 1 for _, radix in stages)
    fx, fk, inv = (jnp.asarray(t) for t in dft_tables(rows))
    flat = jax.ShapeDtypeStruct((rows, chans), jnp.bfloat16)
    vmem = pl.BlockSpec(memory_space=pltpu.VMEM)
    dma = pltpu.SemaphoreType.DMA
    f32, b16 = jnp.float32, jnp.bfloat16
    return pl.pallas_call(
        functools.partial(kernel, ctx_count, ch_count),
        out_shape=(flat, flat),
        in_specs=[vmem] * 11,
        out_specs=(vmem, vmem),
        scratch_shapes=[
            pltpu.VMEM((modes, chans), f32),
            pltpu.VMEM((2 * rows, chans), b16),
            pltpu.VMEM((rows, chans), f32),
            pltpu.VMEM((modes, chans), f32),
            pltpu.VMEM((modes, chans), f32),
            pltpu.VMEM((len(stages), modes, chans), b16),
            pltpu.VMEM((slots, modes, chans), b16),
            pltpu.VMEM((rows, chans), b16),
            pltpu.VMEM((rows, chans), b16),
            pltpu.VMEM((rows, chans), b16),
            pltpu.VMEM((rows, chans), b16),
            pltpu.VMEM((rows, chans), f32),
            pltpu.VMEM((rows, chans), f32),
            pltpu.VMEM((rows, chans), b16),
            pltpu.VMEM((rows, LANES), f32),
            pltpu.VMEM((ch_count - 1, rows, LANES), f32),
            dma((2,)),
            dma((chunks,)),
            dma((chunks,)),
            dma((slots,)),
            dma((slots,)),
            dma((ch_count - 1,)),
            dma((ch_count - 1,)),
        ],
        compiler_params=pltpu.CompilerParams(
            collective_id=0, has_side_effects=True, vmem_limit_bytes=40 * 1024 * 1024
        ),
        cost_estimate=pl.CostEstimate(
            flops=4 * 10**9, bytes_accessed=4 * 10**6, transcendentals=10**6
        ),
    )(
        conv_input,
        jnp.transpose(decay_rates),
        jnp.transpose(residues),
        skip_gain[None, :],
        query_rows,
        key_rows,
        value_rows,
        norm_gain[None, :],
        fx,
        fk,
        inv,
    )


def solution(mesh):
    return jax.shard_map(
        per_device,
        mesh=mesh,
        in_specs=(
            P("ctx", "ch"),
            P("ch", None),
            P("ch", None),
            P("ch"),
            P("ctx", "ch"),
            P("ctx", "ch"),
            P("ctx", "ch"),
            P("ch"),
        ),
        out_specs=(P("ctx", "ch"), P("ctx", "ch")),
        check_vma=False,
    )
```

```python
import functools
import math

import jax
import jax.numpy as jnp
import numpy as np
from jax import lax
from jax.experimental import pallas as pl
from jax.experimental.pallas import tpu as pltpu
from jax.sharding import PartitionSpec as P

HD = 128
LANES = 128
GROUP = 8
HEADS_PER_CHUNK = 4
MESH = pl.DeviceIdType.MESH


def scan_stages(count):
    stages = []
    stride = 1
    while stride < count:
        radix = 4 if count // stride >= 4 else 2
        stages.append((stride, radix))
        stride *= radix
    return stages


def split_bf16(value):
    high = value.astype(jnp.bfloat16)
    low = (value - high.astype(jnp.float32)).astype(jnp.bfloat16)
    return high, low


def dft_tables(rows):
    freq = 2 * np.arange(rows, dtype=np.int64)[:, None] + 1
    place = np.arange(rows, dtype=np.int64)[None, :]
    angle = (freq * place % (4 * rows)).astype(np.float64) * (math.pi / (2 * rows))
    forward = np.concatenate([np.cos(angle), -np.sin(angle)], axis=0)
    inverse = forward.T / rows
    return forward.astype(np.float32), inverse.astype(np.float32)


def kernel(
    ctx_count,
    ch_count,
    x_hbm,
    rate_hbm,
    res_hbm,
    skip_hbm,
    q_hbm,
    k_hbm,
    v_hbm,
    gain_hbm,
    fwd_hbm,
    inv_hbm,
    conv_ref,
    out_ref,
    x_ref,
    rate_ref,
    res_ref,
    skip_ref,
    q_ref,
    k_ref,
    v_ref,
    gain_ref,
    fwd_ref,
    inv_ref,
    fx_s,
    fk_s,
    inv_s,
    load_sem,
    weight_s,
    taps_s,
    intra_s,
    state_s,
    enter_s,
    send_s,
    recv_s,
    gated_s,
    prev_k,
    prev_g,
    soft_s,
    own_s,
    norm_s,
    att_s,
    energy_s,
    energy_r,
    k_send,
    k_recv,
    g_send,
    g_recv,
    s_send,
    s_recv,
    e_send,
    e_recv,
):
    loads = {}
    for i, (name, source, target) in enumerate(
        (
            ("rate", rate_hbm, rate_ref),
            ("x", x_hbm, x_ref),
            ("res", res_hbm, res_ref),
            ("fwd", fwd_hbm, fwd_ref),
            ("inv", inv_hbm, inv_ref),
            ("skip", skip_hbm, skip_ref),
            ("v", v_hbm, v_ref),
            ("k", k_hbm, k_ref),
            ("q", q_hbm, q_ref),
            ("gain", gain_hbm, gain_ref),
        )
    ):
        loads[name] = pltpu.make_async_copy(source, target, load_sem.at[i])
        loads[name].start()

    rows, chans = x_ref.shape
    modes = rate_ref.shape[0]
    tiles = chans // LANES
    groups = rows // GROUP
    heads = chans // HD
    chunks = heads // HEADS_PER_CHUNK
    chunk_cols = HEADS_PER_CHUNK * HD
    pos = lax.axis_index("ctx")
    core = lax.axis_index("ch")
    stages = scan_stages(ctx_count)

    offsets = {1}
    for stride, radix in stages:
        offsets |= {stride * m for m in range(1, radix)}
    offsets = sorted({o % ctx_count for o in offsets} | {-o % ctx_count for o in offsets})
    barrier = pltpu.get_barrier_semaphore()
    for o in offsets:
        pl.semaphore_signal(
            barrier, inc=1, device_id={"ctx": lax.rem(pos + o, ctx_count)}, device_id_type=MESH
        )
    for o in range(1, ch_count):
        pl.semaphore_signal(
            barrier, inc=1, device_id={"ch": lax.rem(core + o, ch_count)}, device_id_type=MESH
        )
    pl.semaphore_wait(barrier, len(offsets) + ch_count - 1)

    after = {"ctx": lax.rem(pos + 1, ctx_count)}
    has_after = pos + 1 < ctx_count
    has_before = pos > 0
    early = chunks // 2

    def key_copy(c):
        part = pl.ds(c * chunk_cols, chunk_cols)
        return pltpu.make_async_remote_copy(
            k_hbm.at[:, part],
            prev_k.at[:, part],
            k_send.at[c],
            k_recv.at[c],
            device_id=after,
            device_id_type=MESH,
        )

    def gated_copy(c):
        part = pl.ds(c * chunk_cols, chunk_cols)
        return pltpu.make_async_remote_copy(
            gated_s.at[:, part],
            prev_g.at[:, part],
            g_send.at[c],
            g_recv.at[c],
            device_id=after,
            device_id_type=MESH,
        )

    def state_copy(level, slot, offset):
        return pltpu.make_async_remote_copy(
            send_s.at[level],
            recv_s.at[slot],
            s_send.at[slot],
            s_recv.at[slot],
            device_id={"ctx": lax.rem(pos + offset, ctx_count)},
            device_id_type=MESH,
        )

    @pl.when(has_after)
    def _():
        for c in range(early):
            key_copy(c).start()

    @pl.when(jnp.logical_not(has_before))
    def _():
        prev_k[...] = jnp.zeros_like(prev_k)
        prev_g[...] = jnp.zeros_like(prev_g)

    u_place = lax.broadcasted_iota(jnp.int32, (1, GROUP, LANES), 1).astype(jnp.float32)

    def state_tile(j, carry):
        cols = pl.ds(pl.multiple_of(j * LANES, LANES), LANES)
        rate = rate_ref[:, cols]
        shrink = jnp.exp(-rate)
        weight_s[:, cols] = res_ref[:, cols] * jnp.sqrt((1.0 - shrink) * (1.0 + shrink))
        rate3 = rate[:, None, :]
        step = jnp.broadcast_to(jnp.exp(-GROUP * rate)[:, None, :], (modes, GROUP, LANES))
        x = x_ref[:, cols].astype(jnp.float32)
        total = jnp.broadcast_to(x[None, 0:GROUP], (modes, GROUP, LANES))
        for i in range(1, groups):
            total = total * step + x[None, i * GROUP : (i + 1) * GROUP]
        total = total * jnp.exp(-rate3 * (GROUP - 1.0 - u_place))
        state = jnp.sum(total, axis=1)
        state_s[:, cols] = state
        send_s[0, :, cols] = state.astype(jnp.bfloat16)
        return carry

    loads["rate"].wait()
    loads["res"].wait()
    loads["x"].wait()
    lax.fori_loop(0, tiles, state_tile, 0)

    def start_stage(level, base):
        stride, radix = stages[level]
        for m in range(1, radix):

            @pl.when(pos + m * stride < ctx_count)
            def _(m=m):
                state_copy(level, base + m - 1, m * stride).start()

            @pl.when(pos < m * stride)
            def _(m=m):
                recv_s[base + m - 1] = jnp.zeros(recv_s.shape[1:], recv_s.dtype)

    def wait_stage(level, base):
        stride, radix = stages[level]
        for m in range(1, radix):

            @pl.when(pos >= m * stride)
            def _(m=m):
                state_copy(level, base + m - 1, m * stride).wait_recv()

    def spread(cols, start):
        rate = rate_ref[:, cols]
        step = jnp.broadcast_to(jnp.exp(-GROUP * rate)[:, None, :], (modes, GROUP, LANES))
        term = start[:, None, :] * jnp.exp(-rate[:, None, :] * u_place)
        parts = []
        for i in range(groups):
            parts.append(jnp.sum(term, axis=0))
            if i + 1 < groups:
                term = term * step
        return jnp.concatenate(parts, axis=0)

    start_stage(0, 0)

    def taps_tile(j, carry):
        cols = pl.ds(pl.multiple_of(j * LANES, LANES), LANES)
        high, low = split_bf16(spread(cols, weight_s[:, cols]))
        taps_s[0:rows, cols] = high
        taps_s[rows : 2 * rows, cols] = low
        return carry

    lax.fori_loop(0, tiles, taps_tile, 0)

    wide = 2 * LANES

    def transform_tile(j, carry):
        cols = pl.ds(pl.multiple_of(j * wide, wide), wide)
        x = x_ref[:, cols]
        taps_high = taps_s[0:rows, cols]
        taps_low = taps_s[rows : 2 * rows, cols]
        spec = jnp.dot(
            fx_s[...], jnp.concatenate([x, x], axis=0), preferred_element_type=jnp.float32
        )
        filt = jnp.dot(
            fk_s[...],
            jnp.concatenate([taps_high, taps_low, taps_high], axis=0),
            preferred_element_type=jnp.float32,
        )
        s_re, s_im = spec[:rows], spec[rows:]
        f_re, f_im = filt[:rows], filt[rows:]
        product = jnp.concatenate([s_re * f_re - s_im * f_im, s_re * f_im + s_im * f_re], axis=0)
        high, low = split_bf16(product)
        intra_s[:, cols] = jnp.dot(
            inv_s[...],
            jnp.concatenate([high, low, high], axis=0),
            preferred_element_type=jnp.float32,
        )
        return carry


    base = 0
    for level, (stride, radix) in enumerate(stages):
        wait_stage(level, base)
        last = level + 1 == len(stages)

        def combine_tile(j, carry, level=level, stride=stride, radix=radix, base=base, last=last):
            cols = pl.ds(pl.multiple_of(j * LANES, LANES), LANES)
            rate = rate_ref[:, cols] * float(rows)
            entered = jnp.zeros((modes, LANES), jnp.float32)
            total = state_s[:, cols]
            for m in range(1, radix):
                got = recv_s[base + m - 1, :, cols].astype(jnp.float32)
                entered = entered + jnp.exp(-rate * (m * stride - 1.0)) * got
                if not last:
                    total = total + jnp.exp(-rate * (1.0 * m * stride)) * got
            if level > 0:
                entered = entered + enter_s[:, cols]
            enter_s[:, cols] = entered
            if not last:
                state_s[:, cols] = total
                send_s[level + 1, :, cols] = total.astype(jnp.bfloat16)
            return carry

        lax.fori_loop(0, tiles, combine_tile, 0)
        base += radix - 1
        if not last:
            start_stage(level + 1, base)
        if level == 0:

            @pl.when(has_after)
            def _():
                for c in range(early, chunks):
                    key_copy(c).start()

            loads["fwd"].wait()
            loads["inv"].wait()
            high, low = split_bf16(fwd_ref[...])
            fx_s[...] = jnp.concatenate([high, low], axis=1)
            fk_s[...] = jnp.concatenate([high, high, low], axis=1)
            high, low = split_bf16(inv_ref[...])
            inv_s[...] = jnp.concatenate([high, high, low], axis=1)
            lax.fori_loop(0, chans // wide, transform_tile, 0)
            loads["skip"].wait()
            loads["v"].wait()

    def gated_tile(j, carry):
        cols = pl.ds(pl.multiple_of(j * LANES, LANES), LANES)
        start = weight_s[:, cols] * enter_s[:, cols] * jnp.exp(-rate_ref[:, cols])
        x = x_ref[:, cols].astype(jnp.float32)
        conv = intra_s[:, cols] + spread(cols, start) + skip_ref[:, cols] * x
        conv = conv.astype(jnp.bfloat16)
        conv_ref[:, cols] = conv
        gated = v_ref[:, cols].astype(jnp.float32) * conv.astype(jnp.float32)
        gated_s[:, cols] = gated.astype(jnp.bfloat16)
        return carry

    for c in range(chunks):
        lax.fori_loop(c * HEADS_PER_CHUNK, (c + 1) * HEADS_PER_CHUNK, gated_tile, 0)

        @pl.when(has_after)
        def _(c=c):
            gated_copy(c).start()

    loads["q"].wait()
    loads["k"].wait()
    loads["gain"].wait()

    @pl.when(has_before)
    def _():
        for c in range(chunks):
            key_copy(c).wait_recv()

    q_place = lax.broadcasted_iota(jnp.int32, (rows, rows), 0)
    k_place = lax.broadcasted_iota(jnp.int32, (rows, rows), 1)
    causal = k_place <= q_place
    before_bias = jnp.where(has_before, 0.0, -jnp.inf)
    contract = (((1,), (1,)), ((), ()))

    def weight_head(h, carry):
        cols = pl.ds(pl.multiple_of(h * HD, HD), HD)
        q = q_ref[:, cols]
        scale = HD ** (-0.5)
        old = lax.dot_general(q, prev_k[:, cols], contract, preferred_element_type=jnp.float32)
        new = lax.dot_general(q, k_ref[:, cols], contract, preferred_element_type=jnp.float32)
        old = old * scale + before_bias
        new = jnp.where(causal, new * scale, -jnp.inf)
        top = jnp.max(jnp.maximum(old, new), axis=1, keepdims=True)
        old = jnp.exp(old - top)
        new = jnp.exp(new - top)
        total = jnp.sum(old + new, axis=1, keepdims=True)
        soft_s[:, cols] = old.astype(jnp.bfloat16)
        own_s[:, cols] = jnp.dot(
            new.astype(jnp.bfloat16), gated_s[:, cols], preferred_element_type=jnp.float32
        )
        norm_s[:, cols] = jnp.broadcast_to(1.0 / total, (rows, HD))
        return carry

    lax.fori_loop(0, heads, weight_head, 0)

    energy_s[...] = jnp.zeros_like(energy_s)

    def mix_head(h, carry):
        cols = pl.ds(pl.multiple_of(h * HD, HD), HD)
        mixed = own_s[:, cols] + jnp.dot(
            soft_s[:, cols], prev_g[:, cols], preferred_element_type=jnp.float32
        )
        attention = (mixed * norm_s[:, cols]).astype(jnp.bfloat16)
        att_s[:, cols] = attention
        attention = attention.astype(jnp.float32)
        energy_s[...] += attention * attention
        return carry

    for c in range(chunks):

        @pl.when(has_before)
        def _(c=c):
            gated_copy(c).wait_recv()

        lax.fori_loop(c * HEADS_PER_CHUNK, (c + 1) * HEADS_PER_CHUNK, mix_head, 0)

    def energy_copy(o):
        return pltpu.make_async_remote_copy(
            energy_s,
            energy_r.at[o - 1],
            e_send.at[o - 1],
            e_recv.at[o - 1],
            device_id={"ch": lax.rem(core + o, ch_count)},
            device_id_type=MESH,
        )

    for o in range(1, ch_count):
        energy_copy(o).start()
    energy = energy_s[...]
    for o in range(1, ch_count):
        energy_copy(o).wait_recv()
        energy = energy + energy_r[o - 1]
    mean_square = jnp.sum(energy, axis=1, keepdims=True) / float(chans * ch_count)
    factor = jnp.broadcast_to(lax.rsqrt(mean_square + 1e-6), (rows, LANES))

    def norm_tile(j, carry):
        cols = pl.ds(pl.multiple_of(j * LANES, LANES), LANES)
        attention = att_s[:, cols].astype(jnp.float32)
        out_ref[:, cols] = (attention * gain_ref[:, cols] * factor).astype(jnp.bfloat16)
        return carry

    lax.fori_loop(0, tiles, norm_tile, 0)

    for o in range(1, ch_count):
        energy_copy(o).wait_send()

    @pl.when(has_after)
    def _():
        for c in range(chunks):
            key_copy(c).wait_send()
            gated_copy(c).wait_send()

    base = 0
    for level, (stride, radix) in enumerate(stages):
        for m in range(1, radix):

            @pl.when(pos + m * stride < ctx_count)
            def _(level=level, slot=base + m - 1, offset=m * stride):
                state_copy(level, slot, offset).wait_send()

        base += radix - 1


def per_device(
    conv_input, residues, decay_rates, skip_gain, query_rows, key_rows, value_rows, norm_gain
):
    ctx_count = lax.axis_size("ctx")
    ch_count = lax.axis_size("ch")
    rows, chans = conv_input.shape
    modes = residues.shape[1]
    chunks = chans // (HEADS_PER_CHUNK * HD)
    stages = scan_stages(ctx_count)
    slots = sum(radix - 1 for _, radix in stages)
    fwd, inv = (jnp.asarray(t) for t in dft_tables(rows))
    flat = jax.ShapeDtypeStruct((rows, chans), jnp.bfloat16)
    vmem = pl.BlockSpec(memory_space=pltpu.VMEM)
    hbm = pl.BlockSpec(memory_space=pltpu.HBM)
    dma = pltpu.SemaphoreType.DMA
    f32, b16 = jnp.float32, jnp.bfloat16
    return pl.pallas_call(
        functools.partial(kernel, ctx_count, ch_count),
        out_shape=(flat, flat),
        in_specs=[hbm] * 10,
        out_specs=(vmem, vmem),
        scratch_shapes=[
            pltpu.VMEM((rows, chans), b16),
            pltpu.VMEM((modes, chans), f32),
            pltpu.VMEM((modes, chans), f32),
            pltpu.VMEM((1, chans), f32),
            pltpu.VMEM((rows, chans), b16),
            pltpu.VMEM((rows, chans), b16),
            pltpu.VMEM((rows, chans), b16),
            pltpu.VMEM((1, chans), f32),
            pltpu.VMEM(fwd.shape, f32),
            pltpu.VMEM(inv.shape, f32),
            pltpu.VMEM((2 * rows, 2 * rows), b16),
            pltpu.VMEM((2 * rows, 3 * rows), b16),
            pltpu.VMEM((rows, 6 * rows), b16),
            dma((10,)),
            pltpu.VMEM((modes, chans), f32),
            pltpu.VMEM((2 * rows, chans), b16),
            pltpu.VMEM((rows, chans), f32),
            pltpu.VMEM((modes, chans), f32),
            pltpu.VMEM((modes, chans), f32),
            pltpu.VMEM((len(stages), modes, chans), b16),
            pltpu.VMEM((slots, modes, chans), b16),
            pltpu.VMEM((rows, chans), b16),
            pltpu.VMEM((rows, chans), b16),
            pltpu.VMEM((rows, chans), b16),
            pltpu.VMEM((rows, chans), b16),
            pltpu.VMEM((rows, chans), f32),
            pltpu.VMEM((rows, chans), f32),
            pltpu.VMEM((rows, chans), b16),
            pltpu.VMEM((rows, LANES), f32),
            pltpu.VMEM((ch_count - 1, rows, LANES), f32),
            dma((chunks,)),
            dma((chunks,)),
            dma((chunks,)),
            dma((chunks,)),
            dma((slots,)),
            dma((slots,)),
            dma((ch_count - 1,)),
            dma((ch_count - 1,)),
        ],
        compiler_params=pltpu.CompilerParams(
            collective_id=0, has_side_effects=True, vmem_limit_bytes=63 * 1024 * 1024
        ),
        cost_estimate=pl.CostEstimate(
            flops=4 * 10**9, bytes_accessed=4 * 10**6, transcendentals=10**6
        ),
    )(
        conv_input,
        jnp.transpose(decay_rates),
        jnp.transpose(residues),
        skip_gain[None, :],
        query_rows,
        key_rows,
        value_rows,
        norm_gain[None, :],
        fwd,
        inv,
    )


def solution(mesh):
    return jax.shard_map(
        per_device,
        mesh=mesh,
        in_specs=(
            P("ctx", "ch"),
            P("ch", None),
            P("ch", None),
            P("ch"),
            P("ctx", "ch"),
            P("ctx", "ch"),
            P("ctx", "ch"),
            P("ch"),
        ),
        out_specs=(P("ctx", "ch"), P("ctx", "ch")),
        check_vma=False,
    )
```

```python
import functools
import math

import jax
import jax.numpy as jnp
import numpy as np
from jax import lax
from jax.experimental import pallas as pl
from jax.experimental.pallas import tpu as pltpu
from jax.sharding import PartitionSpec as P

HD = 128
LANES = 128
GROUP = 8
HEADS_PER_CHUNK = 4
MESH = pl.DeviceIdType.MESH


def scan_stages(count):
    stages = []
    stride = 1
    while stride < count:
        radix = 4 if count // stride >= 4 else 2
        stages.append((stride, radix))
        stride *= radix
    return stages


def split_bf16(value):
    high = value.astype(jnp.bfloat16)
    low = (value - high.astype(jnp.float32)).astype(jnp.bfloat16)
    return high, low


def dft_tables(rows):
    freq = 2 * np.arange(rows, dtype=np.int64)[:, None] + 1
    place = np.arange(rows, dtype=np.int64)[None, :]
    angle = (freq * place % (4 * rows)).astype(np.float64) * (math.pi / (2 * rows))
    forward = np.concatenate([np.cos(angle), -np.sin(angle)], axis=0)
    inverse = forward.T / rows
    return forward.astype(np.float32), inverse.astype(np.float32)


def kernel(
    ctx_count,
    ch_count,
    x_hbm,
    rate_hbm,
    res_hbm,
    skip_hbm,
    q_hbm,
    k_hbm,
    v_hbm,
    gain_hbm,
    fwd_hbm,
    inv_hbm,
    conv_ref,
    out_ref,
    x_ref,
    rate_ref,
    res_ref,
    skip_ref,
    q_ref,
    k_ref,
    v_ref,
    gain_ref,
    fwd_ref,
    inv_ref,
    fx_s,
    fk_s,
    inv_s,
    load_sem,
    weight_s,
    taps_s,
    intra_s,
    state_s,
    enter_s,
    send_s,
    recv_s,
    gated_s,
    prev_k,
    prev_g,
    soft_s,
    own_s,
    norm_s,
    att_s,
    energy_s,
    energy_r,
    k_send,
    k_recv,
    g_send,
    g_recv,
    s_send,
    s_recv,
    e_send,
    e_recv,
):
    loads = {}
    for i, (name, source, target) in enumerate(
        (
            ("rate", rate_hbm, rate_ref),
            ("x", x_hbm, x_ref),
            ("res", res_hbm, res_ref),
            ("fwd", fwd_hbm, fwd_ref),
            ("inv", inv_hbm, inv_ref),
            ("skip", skip_hbm, skip_ref),
            ("v", v_hbm, v_ref),
            ("k", k_hbm, k_ref),
            ("q", q_hbm, q_ref),
            ("gain", gain_hbm, gain_ref),
        )
    ):
        loads[name] = pltpu.make_async_copy(source, target, load_sem.at[i])
        loads[name].start()

    rows, chans = x_ref.shape
    modes = rate_ref.shape[0]
    tiles = chans // LANES
    groups = rows // GROUP
    heads = chans // HD
    chunks = heads // HEADS_PER_CHUNK
    chunk_cols = HEADS_PER_CHUNK * HD
    pos = lax.axis_index("ctx")
    core = lax.axis_index("ch")
    stages = scan_stages(ctx_count)

    offsets = {1}
    for stride, radix in stages:
        offsets |= {stride * m for m in range(1, radix)}
    offsets = sorted({o % ctx_count for o in offsets} | {-o % ctx_count for o in offsets})
    barrier = pltpu.get_barrier_semaphore()
    for o in offsets:
        pl.semaphore_signal(
            barrier, inc=1, device_id={"ctx": lax.rem(pos + o, ctx_count)}, device_id_type=MESH
        )
    for o in range(1, ch_count):
        pl.semaphore_signal(
            barrier, inc=1, device_id={"ch": lax.rem(core + o, ch_count)}, device_id_type=MESH
        )
    pl.semaphore_wait(barrier, len(offsets) + ch_count - 1)

    after = {"ctx": lax.rem(pos + 1, ctx_count)}
    has_after = pos + 1 < ctx_count
    has_before = pos > 0
    early = chunks // 2

    def key_copy(c):
        part = pl.ds(c * chunk_cols, chunk_cols)
        return pltpu.make_async_remote_copy(
            k_hbm.at[:, part],
            prev_k.at[:, part],
            k_send.at[c],
            k_recv.at[c],
            device_id=after,
            device_id_type=MESH,
        )

    def gated_copy(c):
        part = pl.ds(c * chunk_cols, chunk_cols)
        return pltpu.make_async_remote_copy(
            gated_s.at[:, part],
            prev_g.at[:, part],
            g_send.at[c],
            g_recv.at[c],
            device_id=after,
            device_id_type=MESH,
        )

    def state_copy(level, slot, offset):
        return pltpu.make_async_remote_copy(
            send_s.at[level],
            recv_s.at[slot],
            s_send.at[slot],
            s_recv.at[slot],
            device_id={"ctx": lax.rem(pos + offset, ctx_count)},
            device_id_type=MESH,
        )

    @pl.when(has_after)
    def _():
        for c in range(early):
            key_copy(c).start()

    @pl.when(jnp.logical_not(has_before))
    def _():
        prev_k[...] = jnp.zeros_like(prev_k)
        prev_g[...] = jnp.zeros_like(prev_g)

    u_place = lax.broadcasted_iota(jnp.int32, (1, GROUP, LANES), 1).astype(jnp.float32)

    def state_tile(j, carry):
        cols = pl.ds(pl.multiple_of(j * LANES, LANES), LANES)
        rate = rate_ref[:, cols]
        shrink = jnp.exp(-rate)
        weight_s[:, cols] = res_ref[:, cols] * jnp.sqrt((1.0 - shrink) * (1.0 + shrink))
        rate3 = rate[:, None, :]
        step = jnp.broadcast_to(jnp.exp(-GROUP * rate)[:, None, :], (modes, GROUP, LANES))
        x = x_ref[:, cols].astype(jnp.float32)
        total = jnp.broadcast_to(x[None, 0:GROUP], (modes, GROUP, LANES))
        for i in range(1, groups):
            total = total * step + x[None, i * GROUP : (i + 1) * GROUP]
        total = total * jnp.exp(-rate3 * (GROUP - 1.0 - u_place))
        state = jnp.sum(total, axis=1)
        state_s[:, cols] = state
        send_s[0, :, cols] = state.astype(jnp.bfloat16)
        return carry

    loads["rate"].wait()
    loads["res"].wait()
    loads["x"].wait()
    lax.fori_loop(0, tiles, state_tile, 0)

    def start_stage(level, base):
        stride, radix = stages[level]
        for m in range(1, radix):

            @pl.when(pos + m * stride < ctx_count)
            def _(m=m):
                state_copy(level, base + m - 1, m * stride).start()

            @pl.when(pos < m * stride)
            def _(m=m):
                recv_s[base + m - 1] = jnp.zeros(recv_s.shape[1:], recv_s.dtype)

    def wait_stage(level, base):
        stride, radix = stages[level]
        for m in range(1, radix):

            @pl.when(pos >= m * stride)
            def _(m=m):
                state_copy(level, base + m - 1, m * stride).wait_recv()

    def spread(cols, start):
        rate = rate_ref[:, cols]
        step = jnp.broadcast_to(jnp.exp(-GROUP * rate)[:, None, :], (modes, GROUP, LANES))
        term = start[:, None, :] * jnp.exp(-rate[:, None, :] * u_place)
        parts = []
        for i in range(groups):
            parts.append(jnp.sum(term, axis=0))
            if i + 1 < groups:
                term = term * step
        return jnp.concatenate(parts, axis=0)

    start_stage(0, 0)

    def taps_tile(j, carry):
        cols = pl.ds(pl.multiple_of(j * LANES, LANES), LANES)
        high, low = split_bf16(spread(cols, weight_s[:, cols]))
        taps_s[0:rows, cols] = high
        taps_s[rows : 2 * rows, cols] = low
        return carry

    lax.fori_loop(0, tiles, taps_tile, 0)

    wide = 2 * LANES

    def transform_part(j):
        cols = pl.ds(pl.multiple_of(j * wide, wide), wide)
        x = x_ref[:, cols]
        taps_high = taps_s[0:rows, cols]
        taps_low = taps_s[rows : 2 * rows, cols]
        spec = jnp.dot(
            fx_s[...], jnp.concatenate([x, x], axis=0), preferred_element_type=jnp.float32
        )
        filt = jnp.dot(
            fk_s[...],
            jnp.concatenate([taps_high, taps_low, taps_high], axis=0),
            preferred_element_type=jnp.float32,
        )
        s_re, s_im = spec[:rows], spec[rows:]
        f_re, f_im = filt[:rows], filt[rows:]
        product = jnp.concatenate([s_re * f_re - s_im * f_im, s_re * f_im + s_im * f_re], axis=0)
        high, low = split_bf16(product)
        return cols, jnp.dot(
            inv_s[...],
            jnp.concatenate([high, low, high], axis=0),
            preferred_element_type=jnp.float32,
        )


    def transform_tile(j, carry):
        for cols, value in [transform_part(2 * j), transform_part(2 * j + 1)]:
            intra_s[:, cols] = value
        return carry

    base = 0
    for level, (stride, radix) in enumerate(stages):
        wait_stage(level, base)
        last = level + 1 == len(stages)

        def combine_tile(j, carry, level=level, stride=stride, radix=radix, base=base, last=last):
            cols = pl.ds(pl.multiple_of(j * LANES, LANES), LANES)
            rate = rate_ref[:, cols] * float(rows)
            entered = jnp.zeros((modes, LANES), jnp.float32)
            total = state_s[:, cols]
            for m in range(1, radix):
                got = recv_s[base + m - 1, :, cols].astype(jnp.float32)
                entered = entered + jnp.exp(-rate * (m * stride - 1.0)) * got
                if not last:
                    total = total + jnp.exp(-rate * (1.0 * m * stride)) * got
            if level > 0:
                entered = entered + enter_s[:, cols]
            enter_s[:, cols] = entered
            if not last:
                state_s[:, cols] = total
                send_s[level + 1, :, cols] = total.astype(jnp.bfloat16)
            return carry

        lax.fori_loop(0, tiles, combine_tile, 0)
        base += radix - 1
        if not last:
            start_stage(level + 1, base)
        if level == 0:

            @pl.when(has_after)
            def _():
                for c in range(early, chunks):
                    key_copy(c).start()

            loads["fwd"].wait()
            loads["inv"].wait()
            high, low = split_bf16(fwd_ref[...])
            fx_s[...] = jnp.concatenate([high, low], axis=1)
            fk_s[...] = jnp.concatenate([high, high, low], axis=1)
            high, low = split_bf16(inv_ref[...])
            inv_s[...] = jnp.concatenate([high, high, low], axis=1)
            lax.fori_loop(0, chans // (2 * wide), transform_tile, 0)
            loads["skip"].wait()
            loads["v"].wait()

    def gated_tile(j, carry):
        cols = pl.ds(pl.multiple_of(j * LANES, LANES), LANES)
        start = weight_s[:, cols] * enter_s[:, cols] * jnp.exp(-rate_ref[:, cols])
        x = x_ref[:, cols].astype(jnp.float32)
        conv = intra_s[:, cols] + spread(cols, start) + skip_ref[:, cols] * x
        conv = conv.astype(jnp.bfloat16)
        conv_ref[:, cols] = conv
        gated = v_ref[:, cols].astype(jnp.float32) * conv.astype(jnp.float32)
        gated_s[:, cols] = gated.astype(jnp.bfloat16)
        return carry

    for c in range(chunks):
        lax.fori_loop(c * HEADS_PER_CHUNK, (c + 1) * HEADS_PER_CHUNK, gated_tile, 0)

        @pl.when(has_after)
        def _(c=c):
            gated_copy(c).start()

    loads["q"].wait()
    loads["k"].wait()
    loads["gain"].wait()

    @pl.when(has_before)
    def _():
        for c in range(chunks):
            key_copy(c).wait_recv()

    q_place = lax.broadcasted_iota(jnp.int32, (rows, rows), 0)
    k_place = lax.broadcasted_iota(jnp.int32, (rows, rows), 1)
    causal = k_place <= q_place
    before_bias = jnp.where(has_before, 0.0, -jnp.inf)
    contract = (((1,), (1,)), ((), ()))

    def weight_chunk(c, carry):
        start = c * chunk_cols
        parts = [
            pl.ds(start + h * HD if isinstance(start, int) else pl.multiple_of(start + h * HD, HD), HD)
            for h in range(HEADS_PER_CHUNK)
        ]
        scale = HD ** (-0.5)
        scores = []
        for cols in parts:
            q = q_ref[:, cols]
            old = lax.dot_general(q, prev_k[:, cols], contract, preferred_element_type=jnp.float32)
            new = lax.dot_general(q, k_ref[:, cols], contract, preferred_element_type=jnp.float32)
            scores.append((old * scale + before_bias, jnp.where(causal, new * scale, -jnp.inf)))
        tops = [jnp.max(jnp.maximum(old, new), axis=1, keepdims=True) for old, new in scores]
        weights = [
            (jnp.exp(old - top), jnp.exp(new - top)) for (old, new), top in zip(scores, tops)
        ]
        totals = [jnp.sum(old + new, axis=1, keepdims=True) for old, new in weights]
        mixes = [
            jnp.dot(new.astype(jnp.bfloat16), gated_s[:, cols], preferred_element_type=jnp.float32)
            for (_, new), cols in zip(weights, parts)
        ]
        for cols, (old, _), total, mix in zip(parts, weights, totals, mixes):
            soft_s[:, cols] = old.astype(jnp.bfloat16)
            own_s[:, cols] = mix
            norm_s[:, cols] = jnp.broadcast_to(1.0 / total, (rows, HD))
        return carry

    lax.fori_loop(0, chunks, weight_chunk, 0)

    energy_s[...] = jnp.zeros_like(energy_s)

    def mix_chunk(c, carry):
        start = c * chunk_cols
        parts = [
            pl.ds(start + h * HD if isinstance(start, int) else pl.multiple_of(start + h * HD, HD), HD)
            for h in range(HEADS_PER_CHUNK)
        ]
        mixes = [
            own_s[:, cols]
            + jnp.dot(soft_s[:, cols], prev_g[:, cols], preferred_element_type=jnp.float32)
            for cols in parts
        ]
        mixes = [(m * norm_s[:, cols]).astype(jnp.bfloat16) for m, cols in zip(mixes, parts)]
        total = energy_s[...]
        for cols, attention in zip(parts, mixes):
            att_s[:, cols] = attention
            attention = attention.astype(jnp.float32)
            total = total + attention * attention
        energy_s[...] = total
        return carry

    for c in range(chunks):

        @pl.when(has_before)
        def _(c=c):
            gated_copy(c).wait_recv()

        mix_chunk(c, 0)

    def energy_copy(o):
        return pltpu.make_async_remote_copy(
            energy_s,
            energy_r.at[o - 1],
            e_send.at[o - 1],
            e_recv.at[o - 1],
            device_id={"ch": lax.rem(core + o, ch_count)},
            device_id_type=MESH,
        )

    for o in range(1, ch_count):
        energy_copy(o).start()
    energy = energy_s[...]
    for o in range(1, ch_count):
        energy_copy(o).wait_recv()
        energy = energy + energy_r[o - 1]
    mean_square = jnp.sum(energy, axis=1, keepdims=True) / float(chans * ch_count)
    factor = jnp.broadcast_to(lax.rsqrt(mean_square + 1e-6), (rows, LANES))

    def norm_tile(j, carry):
        cols = pl.ds(pl.multiple_of(j * LANES, LANES), LANES)
        attention = att_s[:, cols].astype(jnp.float32)
        out_ref[:, cols] = (attention * gain_ref[:, cols] * factor).astype(jnp.bfloat16)
        return carry

    lax.fori_loop(0, tiles, norm_tile, 0)

    for o in range(1, ch_count):
        energy_copy(o).wait_send()

    @pl.when(has_after)
    def _():
        for c in range(chunks):
            key_copy(c).wait_send()
            gated_copy(c).wait_send()

    base = 0
    for level, (stride, radix) in enumerate(stages):
        for m in range(1, radix):

            @pl.when(pos + m * stride < ctx_count)
            def _(level=level, slot=base + m - 1, offset=m * stride):
                state_copy(level, slot, offset).wait_send()

        base += radix - 1


def per_device(
    conv_input, residues, decay_rates, skip_gain, query_rows, key_rows, value_rows, norm_gain
):
    ctx_count = lax.axis_size("ctx")
    ch_count = lax.axis_size("ch")
    rows, chans = conv_input.shape
    modes = residues.shape[1]
    chunks = chans // (HEADS_PER_CHUNK * HD)
    stages = scan_stages(ctx_count)
    slots = sum(radix - 1 for _, radix in stages)
    fwd, inv = (jnp.asarray(t) for t in dft_tables(rows))
    flat = jax.ShapeDtypeStruct((rows, chans), jnp.bfloat16)
    vmem = pl.BlockSpec(memory_space=pltpu.VMEM)
    hbm = pl.BlockSpec(memory_space=pltpu.HBM)
    dma = pltpu.SemaphoreType.DMA
    f32, b16 = jnp.float32, jnp.bfloat16
    return pl.pallas_call(
        functools.partial(kernel, ctx_count, ch_count),
        out_shape=(flat, flat),
        in_specs=[hbm] * 10,
        out_specs=(vmem, vmem),
        scratch_shapes=[
            pltpu.VMEM((rows, chans), b16),
            pltpu.VMEM((modes, chans), f32),
            pltpu.VMEM((modes, chans), f32),
            pltpu.VMEM((1, chans), f32),
            pltpu.VMEM((rows, chans), b16),
            pltpu.VMEM((rows, chans), b16),
            pltpu.VMEM((rows, chans), b16),
            pltpu.VMEM((1, chans), f32),
            pltpu.VMEM(fwd.shape, f32),
            pltpu.VMEM(inv.shape, f32),
            pltpu.VMEM((2 * rows, 2 * rows), b16),
            pltpu.VMEM((2 * rows, 3 * rows), b16),
            pltpu.VMEM((rows, 6 * rows), b16),
            dma((10,)),
            pltpu.VMEM((modes, chans), f32),
            pltpu.VMEM((2 * rows, chans), b16),
            pltpu.VMEM((rows, chans), f32),
            pltpu.VMEM((modes, chans), f32),
            pltpu.VMEM((modes, chans), f32),
            pltpu.VMEM((len(stages), modes, chans), b16),
            pltpu.VMEM((slots, modes, chans), b16),
            pltpu.VMEM((rows, chans), b16),
            pltpu.VMEM((rows, chans), b16),
            pltpu.VMEM((rows, chans), b16),
            pltpu.VMEM((rows, chans), b16),
            pltpu.VMEM((rows, chans), f32),
            pltpu.VMEM((rows, chans), f32),
            pltpu.VMEM((rows, chans), b16),
            pltpu.VMEM((rows, LANES), f32),
            pltpu.VMEM((ch_count - 1, rows, LANES), f32),
            dma((chunks,)),
            dma((chunks,)),
            dma((chunks,)),
            dma((chunks,)),
            dma((slots,)),
            dma((slots,)),
            dma((ch_count - 1,)),
            dma((ch_count - 1,)),
        ],
        compiler_params=pltpu.CompilerParams(
            collective_id=0, has_side_effects=True, vmem_limit_bytes=63 * 1024 * 1024
        ),
        cost_estimate=pl.CostEstimate(
            flops=4 * 10**9, bytes_accessed=4 * 10**6, transcendentals=10**6
        ),
    )(
        conv_input,
        jnp.transpose(decay_rates),
        jnp.transpose(residues),
        skip_gain[None, :],
        query_rows,
        key_rows,
        value_rows,
        norm_gain[None, :],
        fwd,
        inv,
    )


def solution(mesh):
    return jax.shard_map(
        per_device,
        mesh=mesh,
        in_specs=(
            P("ctx", "ch"),
            P("ch", None),
            P("ch", None),
            P("ch"),
            P("ctx", "ch"),
            P("ctx", "ch"),
            P("ctx", "ch"),
            P("ch"),
        ),
        out_specs=(P("ctx", "ch"), P("ctx", "ch")),
        check_vma=False,
    )
```

```python
import functools
import math

import jax
import jax.numpy as jnp
import numpy as np
from jax import lax
from jax.experimental import pallas as pl
from jax.experimental.pallas import tpu as pltpu
from jax.sharding import PartitionSpec as P

HD = 128
LANES = 128
GROUP = 8
HEADS_PER_CHUNK = 4
MESH = pl.DeviceIdType.MESH


def scan_stages(count):
    stages = []
    stride = 1
    while stride < count:
        radix = 4 if count // stride >= 4 else 2
        stages.append((stride, radix))
        stride *= radix
    return stages


def split_bf16(value):
    high = value.astype(jnp.bfloat16)
    low = (value - high.astype(jnp.float32)).astype(jnp.bfloat16)
    return high, low


def dft_tables(rows):
    freq = 2 * np.arange(rows, dtype=np.int64)[:, None] + 1
    place = np.arange(rows, dtype=np.int64)[None, :]
    angle = (freq * place % (4 * rows)).astype(np.float64) * (math.pi / (2 * rows))
    forward = np.concatenate([np.cos(angle), -np.sin(angle)], axis=0)
    inverse = forward.T / rows
    return forward.astype(np.float32), inverse.astype(np.float32)


def kernel(
    ctx_count,
    ch_count,
    x_hbm,
    rate_hbm,
    res_hbm,
    skip_hbm,
    q_hbm,
    k_hbm,
    v_hbm,
    gain_hbm,
    fwd_hbm,
    inv_hbm,
    conv_ref,
    out_ref,
    x_ref,
    rate_ref,
    res_ref,
    skip_ref,
    q_ref,
    k_ref,
    v_ref,
    gain_ref,
    fwd_ref,
    inv_ref,
    fx_s,
    fk_s,
    inv_s,
    load_sem,
    weight_s,
    taps_s,
    intra_s,
    state_s,
    enter_s,
    send_s,
    recv_s,
    gated_s,
    prev_k,
    prev_g,
    soft_s,
    own_s,
    norm_s,
    att_s,
    energy_s,
    energy_r,
    k_send,
    k_recv,
    g_send,
    g_recv,
    s_send,
    s_recv,
    e_send,
    e_recv,
):
    loads = {}
    for i, (name, source, target) in enumerate(
        (
            ("rate", rate_hbm, rate_ref),
            ("x", x_hbm, x_ref),
            ("res", res_hbm, res_ref),
            ("fwd", fwd_hbm, fwd_ref),
            ("inv", inv_hbm, inv_ref),
            ("skip", skip_hbm, skip_ref),
            ("v", v_hbm, v_ref),
            ("k", k_hbm, k_ref),
            ("q", q_hbm, q_ref),
            ("gain", gain_hbm, gain_ref),
        )
    ):
        loads[name] = pltpu.make_async_copy(source, target, load_sem.at[i])
        loads[name].start()

    rows, chans = x_ref.shape
    modes = rate_ref.shape[0]
    tiles = chans // LANES
    groups = rows // GROUP
    heads = chans // HD
    chunks = heads // HEADS_PER_CHUNK
    chunk_cols = HEADS_PER_CHUNK * HD
    pos = lax.axis_index("ctx")
    core = lax.axis_index("ch")
    stages = scan_stages(ctx_count)

    offsets = {1}
    for stride, radix in stages:
        offsets |= {stride * m for m in range(1, radix)}
    offsets = sorted({o % ctx_count for o in offsets} | {-o % ctx_count for o in offsets})
    barrier = pltpu.get_barrier_semaphore()
    for o in offsets:
        pl.semaphore_signal(
            barrier, inc=1, device_id={"ctx": lax.rem(pos + o, ctx_count)}, device_id_type=MESH
        )
    for o in range(1, ch_count):
        pl.semaphore_signal(
            barrier, inc=1, device_id={"ch": lax.rem(core + o, ch_count)}, device_id_type=MESH
        )
    pl.semaphore_wait(barrier, len(offsets) + ch_count - 1)

    after = {"ctx": lax.rem(pos + 1, ctx_count)}
    has_after = pos + 1 < ctx_count
    has_before = pos > 0
    early = chunks

    def key_copy(c):
        part = pl.ds(c * chunk_cols, chunk_cols)
        return pltpu.make_async_remote_copy(
            k_hbm.at[:, part],
            prev_k.at[:, part],
            k_send.at[c],
            k_recv.at[c],
            device_id=after,
            device_id_type=MESH,
        )

    def gated_copy(c):
        part = pl.ds(c * chunk_cols, chunk_cols)
        return pltpu.make_async_remote_copy(
            gated_s.at[:, part],
            prev_g.at[:, part],
            g_send.at[c],
            g_recv.at[c],
            device_id=after,
            device_id_type=MESH,
        )

    def state_copy(level, slot, offset):
        return pltpu.make_async_remote_copy(
            send_s.at[level],
            recv_s.at[slot],
            s_send.at[slot],
            s_recv.at[slot],
            device_id={"ctx": lax.rem(pos + offset, ctx_count)},
            device_id_type=MESH,
        )

    @pl.when(has_after)
    def _():
        for c in range(early):
            key_copy(c).start()

    @pl.when(jnp.logical_not(has_before))
    def _():
        prev_k[...] = jnp.zeros_like(prev_k)
        prev_g[...] = jnp.zeros_like(prev_g)

    u_place = lax.broadcasted_iota(jnp.int32, (1, GROUP, LANES), 1).astype(jnp.float32)

    def state_tile(j, carry):
        cols = pl.ds(pl.multiple_of(j * LANES, LANES), LANES)
        rate = rate_ref[:, cols]
        shrink = jnp.exp(-rate)
        weight_s[:, cols] = res_ref[:, cols] * jnp.sqrt((1.0 - shrink) * (1.0 + shrink))
        rate3 = rate[:, None, :]
        step = jnp.broadcast_to(jnp.exp(-GROUP * rate)[:, None, :], (modes, GROUP, LANES))
        x = x_ref[:, cols].astype(jnp.float32)
        total = jnp.broadcast_to(x[None, 0:GROUP], (modes, GROUP, LANES))
        for i in range(1, groups):
            total = total * step + x[None, i * GROUP : (i + 1) * GROUP]
        total = total * jnp.exp(-rate3 * (GROUP - 1.0 - u_place))
        state = jnp.sum(total, axis=1)
        state_s[:, cols] = state
        send_s[0, :, cols] = state.astype(jnp.bfloat16)
        return carry

    loads["rate"].wait()
    loads["res"].wait()
    loads["x"].wait()
    lax.fori_loop(0, tiles, state_tile, 0)

    def start_stage(level, base):
        stride, radix = stages[level]
        for m in range(1, radix):

            @pl.when(pos + m * stride < ctx_count)
            def _(m=m):
                state_copy(level, base + m - 1, m * stride).start()

            @pl.when(pos < m * stride)
            def _(m=m):
                recv_s[base + m - 1] = jnp.zeros(recv_s.shape[1:], recv_s.dtype)

    def wait_stage(level, base):
        stride, radix = stages[level]
        for m in range(1, radix):

            @pl.when(pos >= m * stride)
            def _(m=m):
                state_copy(level, base + m - 1, m * stride).wait_recv()

    def spread(cols, start):
        rate = rate_ref[:, cols]
        step = jnp.broadcast_to(jnp.exp(-GROUP * rate)[:, None, :], (modes, GROUP, LANES))
        term = start[:, None, :] * jnp.exp(-rate[:, None, :] * u_place)
        parts = []
        for i in range(groups):
            parts.append(jnp.sum(term, axis=0))
            if i + 1 < groups:
                term = term * step
        return jnp.concatenate(parts, axis=0)

    start_stage(0, 0)

    def taps_tile(j, carry):
        cols = pl.ds(pl.multiple_of(j * LANES, LANES), LANES)
        high, low = split_bf16(spread(cols, weight_s[:, cols]))
        taps_s[0:rows, cols] = high
        taps_s[rows : 2 * rows, cols] = low
        return carry

    lax.fori_loop(0, tiles, taps_tile, 0)

    wide = 2 * LANES

    def transform_part(j):
        cols = pl.ds(pl.multiple_of(j * wide, wide), wide)
        x = x_ref[:, cols]
        taps_high = taps_s[0:rows, cols]
        taps_low = taps_s[rows : 2 * rows, cols]
        spec = jnp.dot(
            fx_s[...], jnp.concatenate([x, x], axis=0), preferred_element_type=jnp.float32
        )
        filt = jnp.dot(
            fk_s[...],
            jnp.concatenate([taps_high, taps_low, taps_high], axis=0),
            preferred_element_type=jnp.float32,
        )
        s_re, s_im = spec[:rows], spec[rows:]
        f_re, f_im = filt[:rows], filt[rows:]
        product = jnp.concatenate([s_re * f_re - s_im * f_im, s_re * f_im + s_im * f_re], axis=0)
        high, low = split_bf16(product)
        return cols, jnp.dot(
            inv_s[...],
            jnp.concatenate([high, low, high], axis=0),
            preferred_element_type=jnp.float32,
        )


    def transform_tile(j, carry):
        for cols, value in [transform_part(2 * j), transform_part(2 * j + 1)]:
            intra_s[:, cols] = value
        return carry

    base = 0
    for level, (stride, radix) in enumerate(stages):
        wait_stage(level, base)
        last = level + 1 == len(stages)

        def combine_tile(j, carry, level=level, stride=stride, radix=radix, base=base, last=last):
            cols = pl.ds(pl.multiple_of(j * LANES, LANES), LANES)
            rate = rate_ref[:, cols] * float(rows)
            entered = jnp.zeros((modes, LANES), jnp.float32)
            total = state_s[:, cols]
            for m in range(1, radix):
                got = recv_s[base + m - 1, :, cols].astype(jnp.float32)
                entered = entered + jnp.exp(-rate * (m * stride - 1.0)) * got
                if not last:
                    total = total + jnp.exp(-rate * (1.0 * m * stride)) * got
            if level > 0:
                entered = entered + enter_s[:, cols]
            enter_s[:, cols] = entered
            if not last:
                state_s[:, cols] = total
                send_s[level + 1, :, cols] = total.astype(jnp.bfloat16)
            return carry

        lax.fori_loop(0, tiles, combine_tile, 0)
        base += radix - 1
        if not last:
            start_stage(level + 1, base)
        if level == 0:

            @pl.when(has_after)
            def _():
                for c in range(early, chunks):
                    key_copy(c).start()

            loads["fwd"].wait()
            loads["inv"].wait()
            high, low = split_bf16(fwd_ref[...])
            fx_s[...] = jnp.concatenate([high, low], axis=1)
            fk_s[...] = jnp.concatenate([high, high, low], axis=1)
            high, low = split_bf16(inv_ref[...])
            inv_s[...] = jnp.concatenate([high, high, low], axis=1)
            lax.fori_loop(0, chans // (2 * wide), transform_tile, 0)
            loads["skip"].wait()
            loads["v"].wait()

    def gated_tile(j, carry):
        cols = pl.ds(pl.multiple_of(j * LANES, LANES), LANES)
        start = weight_s[:, cols] * enter_s[:, cols] * jnp.exp(-rate_ref[:, cols])
        x = x_ref[:, cols].astype(jnp.float32)
        conv = intra_s[:, cols] + spread(cols, start) + skip_ref[:, cols] * x
        conv = conv.astype(jnp.bfloat16)
        conv_ref[:, cols] = conv
        gated = v_ref[:, cols].astype(jnp.float32) * conv.astype(jnp.float32)
        gated_s[:, cols] = gated.astype(jnp.bfloat16)
        return carry

    for c in range(chunks):
        lax.fori_loop(c * HEADS_PER_CHUNK, (c + 1) * HEADS_PER_CHUNK, gated_tile, 0)

        @pl.when(has_after)
        def _(c=c):
            gated_copy(c).start()

    loads["q"].wait()
    loads["k"].wait()
    loads["gain"].wait()

    @pl.when(has_before)
    def _():
        for c in range(chunks):
            key_copy(c).wait_recv()

    q_place = lax.broadcasted_iota(jnp.int32, (rows, rows), 0)
    k_place = lax.broadcasted_iota(jnp.int32, (rows, rows), 1)
    causal = k_place <= q_place
    before_bias = jnp.where(has_before, 0.0, -jnp.inf)
    contract = (((1,), (1,)), ((), ()))

    def weight_chunk(c, carry):
        start = c * chunk_cols
        parts = [
            pl.ds(start + h * HD if isinstance(start, int) else pl.multiple_of(start + h * HD, HD), HD)
            for h in range(HEADS_PER_CHUNK)
        ]
        scale = HD ** (-0.5)
        scores = []
        for cols in parts:
            q = q_ref[:, cols]
            old = lax.dot_general(q, prev_k[:, cols], contract, preferred_element_type=jnp.float32)
            new = lax.dot_general(q, k_ref[:, cols], contract, preferred_element_type=jnp.float32)
            scores.append((old * scale + before_bias, jnp.where(causal, new * scale, -jnp.inf)))
        tops = [jnp.max(jnp.maximum(old, new), axis=1, keepdims=True) for old, new in scores]
        weights = [
            (jnp.exp(old - top), jnp.exp(new - top)) for (old, new), top in zip(scores, tops)
        ]
        totals = [jnp.sum(old + new, axis=1, keepdims=True) for old, new in weights]
        mixes = [
            jnp.dot(new.astype(jnp.bfloat16), gated_s[:, cols], preferred_element_type=jnp.float32)
            for (_, new), cols in zip(weights, parts)
        ]
        for cols, (old, _), total, mix in zip(parts, weights, totals, mixes):
            soft_s[:, cols] = old.astype(jnp.bfloat16)
            own_s[:, cols] = mix
            norm_s[:, cols] = jnp.broadcast_to(1.0 / total, (rows, HD))
        return carry

    lax.fori_loop(0, chunks, weight_chunk, 0)

    energy_s[...] = jnp.zeros_like(energy_s)

    def mix_chunk(c, carry):
        start = c * chunk_cols
        parts = [
            pl.ds(start + h * HD if isinstance(start, int) else pl.multiple_of(start + h * HD, HD), HD)
            for h in range(HEADS_PER_CHUNK)
        ]
        mixes = [
            own_s[:, cols]
            + jnp.dot(soft_s[:, cols], prev_g[:, cols], preferred_element_type=jnp.float32)
            for cols in parts
        ]
        mixes = [(m * norm_s[:, cols]).astype(jnp.bfloat16) for m, cols in zip(mixes, parts)]
        total = energy_s[...]
        for cols, attention in zip(parts, mixes):
            att_s[:, cols] = attention
            attention = attention.astype(jnp.float32)
            total = total + attention * attention
        energy_s[...] = total
        return carry

    for c in range(chunks):

        @pl.when(has_before)
        def _(c=c):
            gated_copy(c).wait_recv()

        mix_chunk(c, 0)

    def energy_copy(o):
        return pltpu.make_async_remote_copy(
            energy_s,
            energy_r.at[o - 1],
            e_send.at[o - 1],
            e_recv.at[o - 1],
            device_id={"ch": lax.rem(core + o, ch_count)},
            device_id_type=MESH,
        )

    for o in range(1, ch_count):
        energy_copy(o).start()
    energy = energy_s[...]
    for o in range(1, ch_count):
        energy_copy(o).wait_recv()
        energy = energy + energy_r[o - 1]
    mean_square = jnp.sum(energy, axis=1, keepdims=True) / float(chans * ch_count)
    factor = jnp.broadcast_to(lax.rsqrt(mean_square + 1e-6), (rows, LANES))

    def norm_tile(j, carry):
        cols = pl.ds(pl.multiple_of(j * LANES, LANES), LANES)
        attention = att_s[:, cols].astype(jnp.float32)
        out_ref[:, cols] = (attention * gain_ref[:, cols] * factor).astype(jnp.bfloat16)
        return carry

    lax.fori_loop(0, tiles, norm_tile, 0)

    for o in range(1, ch_count):
        energy_copy(o).wait_send()

    @pl.when(has_after)
    def _():
        for c in range(chunks):
            key_copy(c).wait_send()
            gated_copy(c).wait_send()

    base = 0
    for level, (stride, radix) in enumerate(stages):
        for m in range(1, radix):

            @pl.when(pos + m * stride < ctx_count)
            def _(level=level, slot=base + m - 1, offset=m * stride):
                state_copy(level, slot, offset).wait_send()

        base += radix - 1


def per_device(
    conv_input, residues, decay_rates, skip_gain, query_rows, key_rows, value_rows, norm_gain
):
    ctx_count = lax.axis_size("ctx")
    ch_count = lax.axis_size("ch")
    rows, chans = conv_input.shape
    modes = residues.shape[1]
    chunks = chans // (HEADS_PER_CHUNK * HD)
    stages = scan_stages(ctx_count)
    slots = sum(radix - 1 for _, radix in stages)
    fwd, inv = (jnp.asarray(t) for t in dft_tables(rows))
    flat = jax.ShapeDtypeStruct((rows, chans), jnp.bfloat16)
    vmem = pl.BlockSpec(memory_space=pltpu.VMEM)
    hbm = pl.BlockSpec(memory_space=pltpu.HBM)
    dma = pltpu.SemaphoreType.DMA
    f32, b16 = jnp.float32, jnp.bfloat16
    return pl.pallas_call(
        functools.partial(kernel, ctx_count, ch_count),
        out_shape=(flat, flat),
        in_specs=[hbm] * 10,
        out_specs=(vmem, vmem),
        scratch_shapes=[
            pltpu.VMEM((rows, chans), b16),
            pltpu.VMEM((modes, chans), f32),
            pltpu.VMEM((modes, chans), f32),
            pltpu.VMEM((1, chans), f32),
            pltpu.VMEM((rows, chans), b16),
            pltpu.VMEM((rows, chans), b16),
            pltpu.VMEM((rows, chans), b16),
            pltpu.VMEM((1, chans), f32),
            pltpu.VMEM(fwd.shape, f32),
            pltpu.VMEM(inv.shape, f32),
            pltpu.VMEM((2 * rows, 2 * rows), b16),
            pltpu.VMEM((2 * rows, 3 * rows), b16),
            pltpu.VMEM((rows, 6 * rows), b16),
            dma((10,)),
            pltpu.VMEM((modes, chans), f32),
            pltpu.VMEM((2 * rows, chans), b16),
            pltpu.VMEM((rows, chans), f32),
            pltpu.VMEM((modes, chans), f32),
            pltpu.VMEM((modes, chans), f32),
            pltpu.VMEM((len(stages), modes, chans), b16),
            pltpu.VMEM((slots, modes, chans), b16),
            pltpu.VMEM((rows, chans), b16),
            pltpu.VMEM((rows, chans), b16),
            pltpu.VMEM((rows, chans), b16),
            pltpu.VMEM((rows, chans), b16),
            pltpu.VMEM((rows, chans), f32),
            pltpu.VMEM((rows, chans), f32),
            pltpu.VMEM((rows, chans), b16),
            pltpu.VMEM((rows, LANES), f32),
            pltpu.VMEM((ch_count - 1, rows, LANES), f32),
            dma((chunks,)),
            dma((chunks,)),
            dma((chunks,)),
            dma((chunks,)),
            dma((slots,)),
            dma((slots,)),
            dma((ch_count - 1,)),
            dma((ch_count - 1,)),
        ],
        compiler_params=pltpu.CompilerParams(
            collective_id=0, has_side_effects=True, vmem_limit_bytes=63 * 1024 * 1024
        ),
        cost_estimate=pl.CostEstimate(
            flops=4 * 10**9, bytes_accessed=4 * 10**6, transcendentals=10**6
        ),
    )(
        conv_input,
        jnp.transpose(decay_rates),
        jnp.transpose(residues),
        skip_gain[None, :],
        query_rows,
        key_rows,
        value_rows,
        norm_gain[None, :],
        fwd,
        inv,
    )


def solution(mesh):
    return jax.shard_map(
        per_device,
        mesh=mesh,
        in_specs=(
            P("ctx", "ch"),
            P("ch", None),
            P("ch", None),
            P("ch"),
            P("ctx", "ch"),
            P("ctx", "ch"),
            P("ctx", "ch"),
            P("ch"),
        ),
        out_specs=(P("ctx", "ch"), P("ctx", "ch")),
        check_vma=False,
    )
```

```python
import functools
import math

import jax
import jax.numpy as jnp
import numpy as np
from jax import lax
from jax.experimental import pallas as pl
from jax.experimental.pallas import tpu as pltpu
from jax.sharding import PartitionSpec as P

HD = 128
LANES = 128
GROUP = 8
HEADS_PER_CHUNK = 4
MESH = pl.DeviceIdType.MESH


def scan_stages(count):
    stages = []
    stride = 1
    while stride < count:
        radix = 4 if count // stride >= 4 else 2
        stages.append((stride, radix))
        stride *= radix
    return stages


def split_bf16(value):
    high = value.astype(jnp.bfloat16)
    low = (value - high.astype(jnp.float32)).astype(jnp.bfloat16)
    return high, low


def dft_tables(rows):
    freq = 2 * np.arange(rows, dtype=np.int64)[:, None] + 1
    place = np.arange(rows, dtype=np.int64)[None, :]
    angle = (freq * place % (4 * rows)).astype(np.float64) * (math.pi / (2 * rows))
    forward = np.concatenate([np.cos(angle), -np.sin(angle)], axis=0)
    inverse = forward.T / rows
    return forward.astype(np.float32), inverse.astype(np.float32)


def kernel(
    ctx_count,
    ch_count,
    x_hbm,
    rate_hbm,
    res_hbm,
    skip_hbm,
    q_hbm,
    k_hbm,
    v_hbm,
    gain_hbm,
    fwd_hbm,
    inv_hbm,
    conv_ref,
    out_ref,
    x_ref,
    rate_ref,
    res_ref,
    skip_ref,
    q_ref,
    k_ref,
    v_ref,
    gain_ref,
    fwd_ref,
    inv_ref,
    fx_s,
    fk_s,
    inv_s,
    load_sem,
    weight_s,
    taps_s,
    intra_s,
    state_s,
    enter_s,
    send_s,
    recv_s,
    gated_s,
    prev_k,
    prev_g,
    soft_s,
    own_s,
    norm_s,
    att_s,
    energy_s,
    energy_r,
    k_send,
    k_recv,
    g_send,
    g_recv,
    s_send,
    s_recv,
    e_send,
    e_recv,
):
    loads = {}
    for i, (name, source, target) in enumerate(
        (
            ("rate", rate_hbm, rate_ref),
            ("x", x_hbm, x_ref),
            ("res", res_hbm, res_ref),
            ("fwd", fwd_hbm, fwd_ref),
            ("inv", inv_hbm, inv_ref),
            ("skip", skip_hbm, skip_ref),
            ("v", v_hbm, v_ref),
            ("k", k_hbm, k_ref),
            ("q", q_hbm, q_ref),
            ("gain", gain_hbm, gain_ref),
        )
    ):
        loads[name] = pltpu.make_async_copy(source, target, load_sem.at[i])
        loads[name].start()

    rows, chans = x_ref.shape
    modes = rate_ref.shape[0]
    tiles = chans // LANES
    groups = rows // GROUP
    heads = chans // HD
    chunks = heads // HEADS_PER_CHUNK
    chunk_cols = HEADS_PER_CHUNK * HD
    pos = lax.axis_index("ctx")
    core = lax.axis_index("ch")
    stages = scan_stages(ctx_count)

    offsets = {1}
    for stride, radix in stages:
        offsets |= {stride * m for m in range(1, radix)}
    offsets = sorted({o % ctx_count for o in offsets} | {-o % ctx_count for o in offsets})
    barrier = pltpu.get_barrier_semaphore()
    for o in offsets:
        pl.semaphore_signal(
            barrier, inc=1, device_id={"ctx": lax.rem(pos + o, ctx_count)}, device_id_type=MESH
        )
    for o in range(1, ch_count):
        pl.semaphore_signal(
            barrier, inc=1, device_id={"ch": lax.rem(core + o, ch_count)}, device_id_type=MESH
        )
    pl.semaphore_wait(barrier, len(offsets) + ch_count - 1)

    after = {"ctx": lax.rem(pos + 1, ctx_count)}
    has_after = pos + 1 < ctx_count
    has_before = pos > 0
    early = chunks // 4

    def key_copy(c):
        part = pl.ds(c * chunk_cols, chunk_cols)
        return pltpu.make_async_remote_copy(
            k_hbm.at[:, part],
            prev_k.at[:, part],
            k_send.at[c],
            k_recv.at[c],
            device_id=after,
            device_id_type=MESH,
        )

    def gated_copy(c):
        part = pl.ds(c * chunk_cols, chunk_cols)
        return pltpu.make_async_remote_copy(
            gated_s.at[:, part],
            prev_g.at[:, part],
            g_send.at[c],
            g_recv.at[c],
            device_id=after,
            device_id_type=MESH,
        )

    def state_copy(level, slot, offset):
        return pltpu.make_async_remote_copy(
            send_s.at[level],
            recv_s.at[slot],
            s_send.at[slot],
            s_recv.at[slot],
            device_id={"ctx": lax.rem(pos + offset, ctx_count)},
            device_id_type=MESH,
        )

    @pl.when(has_after)
    def _():
        for c in range(early):
            key_copy(c).start()

    @pl.when(jnp.logical_not(has_before))
    def _():
        prev_k[...] = jnp.zeros_like(prev_k)
        prev_g[...] = jnp.zeros_like(prev_g)

    u_place = lax.broadcasted_iota(jnp.int32, (1, GROUP, LANES), 1).astype(jnp.float32)

    def state_tile(j, carry):
        cols = pl.ds(pl.multiple_of(j * LANES, LANES), LANES)
        rate = rate_ref[:, cols]
        shrink = jnp.exp(-rate)
        weight_s[:, cols] = res_ref[:, cols] * jnp.sqrt((1.0 - shrink) * (1.0 + shrink))
        rate3 = rate[:, None, :]
        step = jnp.broadcast_to(jnp.exp(-GROUP * rate)[:, None, :], (modes, GROUP, LANES))
        x = x_ref[:, cols].astype(jnp.float32)
        total = jnp.broadcast_to(x[None, 0:GROUP], (modes, GROUP, LANES))
        for i in range(1, groups):
            total = total * step + x[None, i * GROUP : (i + 1) * GROUP]
        total = total * jnp.exp(-rate3 * (GROUP - 1.0 - u_place))
        state = jnp.sum(total, axis=1)
        state_s[:, cols] = state
        send_s[0, :, cols] = state.astype(jnp.bfloat16)
        return carry

    loads["rate"].wait()
    loads["res"].wait()
    loads["x"].wait()
    lax.fori_loop(0, tiles, state_tile, 0)

    def start_stage(level, base):
        stride, radix = stages[level]
        for m in range(1, radix):

            @pl.when(pos + m * stride < ctx_count)
            def _(m=m):
                state_copy(level, base + m - 1, m * stride).start()

            @pl.when(pos < m * stride)
            def _(m=m):
                recv_s[base + m - 1] = jnp.zeros(recv_s.shape[1:], recv_s.dtype)

    def wait_stage(level, base):
        stride, radix = stages[level]
        for m in range(1, radix):

            @pl.when(pos >= m * stride)
            def _(m=m):
                state_copy(level, base + m - 1, m * stride).wait_recv()

    def spread(cols, start):
        rate = rate_ref[:, cols]
        step = jnp.broadcast_to(jnp.exp(-GROUP * rate)[:, None, :], (modes, GROUP, LANES))
        term = start[:, None, :] * jnp.exp(-rate[:, None, :] * u_place)
        parts = []
        for i in range(groups):
            parts.append(jnp.sum(term, axis=0))
            if i + 1 < groups:
                term = term * step
        return jnp.concatenate(parts, axis=0)

    start_stage(0, 0)

    def taps_tile(j, carry):
        cols = pl.ds(pl.multiple_of(j * LANES, LANES), LANES)
        high, low = split_bf16(spread(cols, weight_s[:, cols]))
        taps_s[0:rows, cols] = high
        taps_s[rows : 2 * rows, cols] = low
        return carry

    lax.fori_loop(0, tiles, taps_tile, 0)

    wide = 2 * LANES

    def transform_part(j):
        cols = pl.ds(pl.multiple_of(j * wide, wide), wide)
        x = x_ref[:, cols]
        taps_high = taps_s[0:rows, cols]
        taps_low = taps_s[rows : 2 * rows, cols]
        spec = jnp.dot(
            fx_s[...], jnp.concatenate([x, x], axis=0), preferred_element_type=jnp.float32
        )
        filt = jnp.dot(
            fk_s[...],
            jnp.concatenate([taps_high, taps_low, taps_high], axis=0),
            preferred_element_type=jnp.float32,
        )
        s_re, s_im = spec[:rows], spec[rows:]
        f_re, f_im = filt[:rows], filt[rows:]
        product = jnp.concatenate([s_re * f_re - s_im * f_im, s_re * f_im + s_im * f_re], axis=0)
        high, low = split_bf16(product)
        return cols, jnp.dot(
            inv_s[...],
            jnp.concatenate([high, low, high], axis=0),
            preferred_element_type=jnp.float32,
        )


    def transform_tile(j, carry):
        for cols, value in [transform_part(2 * j), transform_part(2 * j + 1)]:
            intra_s[:, cols] = value
        return carry

    base = 0
    for level, (stride, radix) in enumerate(stages):
        wait_stage(level, base)
        last = level + 1 == len(stages)

        def combine_tile(j, carry, level=level, stride=stride, radix=radix, base=base, last=last):
            cols = pl.ds(pl.multiple_of(j * LANES, LANES), LANES)
            rate = rate_ref[:, cols] * float(rows)
            entered = jnp.zeros((modes, LANES), jnp.float32)
            total = state_s[:, cols]
            for m in range(1, radix):
                got = recv_s[base + m - 1, :, cols].astype(jnp.float32)
                entered = entered + jnp.exp(-rate * (m * stride - 1.0)) * got
                if not last:
                    total = total + jnp.exp(-rate * (1.0 * m * stride)) * got
            if level > 0:
                entered = entered + enter_s[:, cols]
            enter_s[:, cols] = entered
            if not last:
                state_s[:, cols] = total
                send_s[level + 1, :, cols] = total.astype(jnp.bfloat16)
            return carry

        lax.fori_loop(0, tiles, combine_tile, 0)
        base += radix - 1
        if not last:
            start_stage(level + 1, base)
        if level == 0:

            @pl.when(has_after)
            def _():
                for c in range(early, chunks):
                    key_copy(c).start()

            loads["fwd"].wait()
            loads["inv"].wait()
            high, low = split_bf16(fwd_ref[...])
            fx_s[...] = jnp.concatenate([high, low], axis=1)
            fk_s[...] = jnp.concatenate([high, high, low], axis=1)
            high, low = split_bf16(inv_ref[...])
            inv_s[...] = jnp.concatenate([high, high, low], axis=1)
            lax.fori_loop(0, chans // (2 * wide), transform_tile, 0)
            loads["skip"].wait()
            loads["v"].wait()

    def gated_tile(j, carry):
        cols = pl.ds(pl.multiple_of(j * LANES, LANES), LANES)
        start = weight_s[:, cols] * enter_s[:, cols] * jnp.exp(-rate_ref[:, cols])
        x = x_ref[:, cols].astype(jnp.float32)
        conv = intra_s[:, cols] + spread(cols, start) + skip_ref[:, cols] * x
        conv = conv.astype(jnp.bfloat16)
        conv_ref[:, cols] = conv
        gated = v_ref[:, cols].astype(jnp.float32) * conv.astype(jnp.float32)
        gated_s[:, cols] = gated.astype(jnp.bfloat16)
        return carry

    for c in range(chunks):
        lax.fori_loop(c * HEADS_PER_CHUNK, (c + 1) * HEADS_PER_CHUNK, gated_tile, 0)

        @pl.when(has_after)
        def _(c=c):
            gated_copy(c).start()

    loads["q"].wait()
    loads["k"].wait()
    loads["gain"].wait()

    @pl.when(has_before)
    def _():
        for c in range(chunks):
            key_copy(c).wait_recv()

    q_place = lax.broadcasted_iota(jnp.int32, (rows, rows), 0)
    k_place = lax.broadcasted_iota(jnp.int32, (rows, rows), 1)
    causal = k_place <= q_place
    before_bias = jnp.where(has_before, 0.0, -jnp.inf)
    contract = (((1,), (1,)), ((), ()))

    def weight_chunk(c, carry):
        start = c * chunk_cols
        parts = [
            pl.ds(start + h * HD if isinstance(start, int) else pl.multiple_of(start + h * HD, HD), HD)
            for h in range(HEADS_PER_CHUNK)
        ]
        scale = HD ** (-0.5)
        scores = []
        for cols in parts:
            q = q_ref[:, cols]
            old = lax.dot_general(q, prev_k[:, cols], contract, preferred_element_type=jnp.float32)
            new = lax.dot_general(q, k_ref[:, cols], contract, preferred_element_type=jnp.float32)
            scores.append((old * scale + before_bias, jnp.where(causal, new * scale, -jnp.inf)))
        tops = [jnp.max(jnp.maximum(old, new), axis=1, keepdims=True) for old, new in scores]
        weights = [
            (jnp.exp(old - top), jnp.exp(new - top)) for (old, new), top in zip(scores, tops)
        ]
        totals = [jnp.sum(old + new, axis=1, keepdims=True) for old, new in weights]
        mixes = [
            jnp.dot(new.astype(jnp.bfloat16), gated_s[:, cols], preferred_element_type=jnp.float32)
            for (_, new), cols in zip(weights, parts)
        ]
        for cols, (old, _), total, mix in zip(parts, weights, totals, mixes):
            soft_s[:, cols] = old.astype(jnp.bfloat16)
            own_s[:, cols] = mix
            norm_s[:, cols] = jnp.broadcast_to(1.0 / total, (rows, HD))
        return carry

    lax.fori_loop(0, chunks, weight_chunk, 0)

    energy_s[...] = jnp.zeros_like(energy_s)

    def mix_chunk(c, carry):
        start = c * chunk_cols
        parts = [
            pl.ds(start + h * HD if isinstance(start, int) else pl.multiple_of(start + h * HD, HD), HD)
            for h in range(HEADS_PER_CHUNK)
        ]
        mixes = [
            own_s[:, cols]
            + jnp.dot(soft_s[:, cols], prev_g[:, cols], preferred_element_type=jnp.float32)
            for cols in parts
        ]
        mixes = [(m * norm_s[:, cols]).astype(jnp.bfloat16) for m, cols in zip(mixes, parts)]
        total = energy_s[...]
        for cols, attention in zip(parts, mixes):
            att_s[:, cols] = attention
            attention = attention.astype(jnp.float32)
            total = total + attention * attention
        energy_s[...] = total
        return carry

    for c in range(chunks):

        @pl.when(has_before)
        def _(c=c):
            gated_copy(c).wait_recv()

        mix_chunk(c, 0)

    def energy_copy(o):
        return pltpu.make_async_remote_copy(
            energy_s,
            energy_r.at[o - 1],
            e_send.at[o - 1],
            e_recv.at[o - 1],
            device_id={"ch": lax.rem(core + o, ch_count)},
            device_id_type=MESH,
        )

    for o in range(1, ch_count):
        energy_copy(o).start()
    energy = energy_s[...]
    for o in range(1, ch_count):
        energy_copy(o).wait_recv()
        energy = energy + energy_r[o - 1]
    mean_square = jnp.sum(energy, axis=1, keepdims=True) / float(chans * ch_count)
    factor = jnp.broadcast_to(lax.rsqrt(mean_square + 1e-6), (rows, LANES))

    def norm_tile(j, carry):
        cols = pl.ds(pl.multiple_of(j * LANES, LANES), LANES)
        attention = att_s[:, cols].astype(jnp.float32)
        out_ref[:, cols] = (attention * gain_ref[:, cols] * factor).astype(jnp.bfloat16)
        return carry

    lax.fori_loop(0, tiles, norm_tile, 0)

    for o in range(1, ch_count):
        energy_copy(o).wait_send()

    @pl.when(has_after)
    def _():
        for c in range(chunks):
            key_copy(c).wait_send()
            gated_copy(c).wait_send()

    base = 0
    for level, (stride, radix) in enumerate(stages):
        for m in range(1, radix):

            @pl.when(pos + m * stride < ctx_count)
            def _(level=level, slot=base + m - 1, offset=m * stride):
                state_copy(level, slot, offset).wait_send()

        base += radix - 1


def per_device(
    conv_input, residues, decay_rates, skip_gain, query_rows, key_rows, value_rows, norm_gain
):
    ctx_count = lax.axis_size("ctx")
    ch_count = lax.axis_size("ch")
    rows, chans = conv_input.shape
    modes = residues.shape[1]
    chunks = chans // (HEADS_PER_CHUNK * HD)
    stages = scan_stages(ctx_count)
    slots = sum(radix - 1 for _, radix in stages)
    fwd, inv = (jnp.asarray(t) for t in dft_tables(rows))
    flat = jax.ShapeDtypeStruct((rows, chans), jnp.bfloat16)
    vmem = pl.BlockSpec(memory_space=pltpu.VMEM)
    hbm = pl.BlockSpec(memory_space=pltpu.HBM)
    dma = pltpu.SemaphoreType.DMA
    f32, b16 = jnp.float32, jnp.bfloat16
    return pl.pallas_call(
        functools.partial(kernel, ctx_count, ch_count),
        out_shape=(flat, flat),
        in_specs=[hbm] * 10,
        out_specs=(vmem, vmem),
        scratch_shapes=[
            pltpu.VMEM((rows, chans), b16),
            pltpu.VMEM((modes, chans), f32),
            pltpu.VMEM((modes, chans), f32),
            pltpu.VMEM((1, chans), f32),
            pltpu.VMEM((rows, chans), b16),
            pltpu.VMEM((rows, chans), b16),
            pltpu.VMEM((rows, chans), b16),
            pltpu.VMEM((1, chans), f32),
            pltpu.VMEM(fwd.shape, f32),
            pltpu.VMEM(inv.shape, f32),
            pltpu.VMEM((2 * rows, 2 * rows), b16),
            pltpu.VMEM((2 * rows, 3 * rows), b16),
            pltpu.VMEM((rows, 6 * rows), b16),
            dma((10,)),
            pltpu.VMEM((modes, chans), f32),
            pltpu.VMEM((2 * rows, chans), b16),
            pltpu.VMEM((rows, chans), f32),
            pltpu.VMEM((modes, chans), f32),
            pltpu.VMEM((modes, chans), f32),
            pltpu.VMEM((len(stages), modes, chans), b16),
            pltpu.VMEM((slots, modes, chans), b16),
            pltpu.VMEM((rows, chans), b16),
            pltpu.VMEM((rows, chans), b16),
            pltpu.VMEM((rows, chans), b16),
            pltpu.VMEM((rows, chans), b16),
            pltpu.VMEM((rows, chans), f32),
            pltpu.VMEM((rows, chans), f32),
            pltpu.VMEM((rows, chans), b16),
            pltpu.VMEM((rows, LANES), f32),
            pltpu.VMEM((ch_count - 1, rows, LANES), f32),
            dma((chunks,)),
            dma((chunks,)),
            dma((chunks,)),
            dma((chunks,)),
            dma((slots,)),
            dma((slots,)),
            dma((ch_count - 1,)),
            dma((ch_count - 1,)),
        ],
        compiler_params=pltpu.CompilerParams(
            collective_id=0, has_side_effects=True, vmem_limit_bytes=63 * 1024 * 1024
        ),
        cost_estimate=pl.CostEstimate(
            flops=4 * 10**9, bytes_accessed=4 * 10**6, transcendentals=10**6
        ),
    )(
        conv_input,
        jnp.transpose(decay_rates),
        jnp.transpose(residues),
        skip_gain[None, :],
        query_rows,
        key_rows,
        value_rows,
        norm_gain[None, :],
        fwd,
        inv,
    )


def solution(mesh):
    return jax.shard_map(
        per_device,
        mesh=mesh,
        in_specs=(
            P("ctx", "ch"),
            P("ch", None),
            P("ch", None),
            P("ch"),
            P("ctx", "ch"),
            P("ctx", "ch"),
            P("ctx", "ch"),
            P("ch"),
        ),
        out_specs=(P("ctx", "ch"), P("ctx", "ch")),
        check_vma=False,
    )
```

```python
import functools
import math

import jax
import jax.numpy as jnp
import numpy as np
from jax import lax
from jax.experimental import pallas as pl
from jax.experimental.pallas import tpu as pltpu
from jax.sharding import PartitionSpec as P

HD = 128
LANES = 128
GROUP = 8
HEADS_PER_CHUNK = 4
MESH = pl.DeviceIdType.MESH


def scan_stages(count):
    stages = []
    stride = 1
    while stride < count:
        radix = 4 if count // stride >= 4 else 2
        stages.append((stride, radix))
        stride *= radix
    return stages


def split_bf16(value):
    high = value.astype(jnp.bfloat16)
    low = (value - high.astype(jnp.float32)).astype(jnp.bfloat16)
    return high, low


def dft_tables(rows):
    freq = 2 * np.arange(rows, dtype=np.int64)[:, None] + 1
    place = np.arange(rows, dtype=np.int64)[None, :]
    angle = (freq * place % (4 * rows)).astype(np.float64) * (math.pi / (2 * rows))
    forward = np.concatenate([np.cos(angle), -np.sin(angle)], axis=0)
    inverse = forward.T / rows
    return forward.astype(np.float32), inverse.astype(np.float32)


def kernel(
    ctx_count,
    ch_count,
    x_hbm,
    rate_hbm,
    res_hbm,
    skip_hbm,
    q_hbm,
    k_hbm,
    v_hbm,
    gain_hbm,
    fwd_hbm,
    inv_hbm,
    conv_ref,
    out_ref,
    x_ref,
    rate_ref,
    res_ref,
    skip_ref,
    q_ref,
    k_ref,
    v_ref,
    gain_ref,
    fwd_ref,
    inv_ref,
    fx_s,
    fk_s,
    inv_s,
    load_sem,
    weight_s,
    taps_s,
    intra_s,
    state_s,
    enter_s,
    send_s,
    recv_s,
    gated_s,
    prev_k,
    prev_g,
    soft_s,
    own_s,
    norm_s,
    att_s,
    energy_s,
    energy_r,
    k_send,
    k_recv,
    g_send,
    g_recv,
    s_send,
    s_recv,
    e_send,
    e_recv,
):
    loads = {}
    for i, (name, source, target) in enumerate(
        (
            ("rate", rate_hbm, rate_ref),
            ("x", x_hbm, x_ref),
            ("res", res_hbm, res_ref),
            ("fwd", fwd_hbm, fwd_ref),
            ("inv", inv_hbm, inv_ref),
            ("skip", skip_hbm, skip_ref),
            ("v", v_hbm, v_ref),
            ("k", k_hbm, k_ref),
            ("q", q_hbm, q_ref),
            ("gain", gain_hbm, gain_ref),
        )
    ):
        loads[name] = pltpu.make_async_copy(source, target, load_sem.at[i])
        loads[name].start()

    rows, chans = x_ref.shape
    modes = rate_ref.shape[0]
    tiles = chans // LANES
    groups = rows // GROUP
    heads = chans // HD
    chunks = heads // HEADS_PER_CHUNK
    chunk_cols = HEADS_PER_CHUNK * HD
    pos = lax.axis_index("ctx")
    core = lax.axis_index("ch")
    stages = scan_stages(ctx_count)

    offsets = {1}
    for stride, radix in stages:
        offsets |= {stride * m for m in range(1, radix)}
    offsets = sorted({o % ctx_count for o in offsets} | {-o % ctx_count for o in offsets})
    barrier = pltpu.get_barrier_semaphore()
    for o in offsets:
        pl.semaphore_signal(
            barrier, inc=1, device_id={"ctx": lax.rem(pos + o, ctx_count)}, device_id_type=MESH
        )
    for o in range(1, ch_count):
        pl.semaphore_signal(
            barrier, inc=1, device_id={"ch": lax.rem(core + o, ch_count)}, device_id_type=MESH
        )
    pl.semaphore_wait(barrier, len(offsets) + ch_count - 1)

    after = {"ctx": lax.rem(pos + 1, ctx_count)}
    has_after = pos + 1 < ctx_count
    has_before = pos > 0
    early = 0

    def key_copy(c):
        part = pl.ds(c * chunk_cols, chunk_cols)
        return pltpu.make_async_remote_copy(
            k_hbm.at[:, part],
            prev_k.at[:, part],
            k_send.at[c],
            k_recv.at[c],
            device_id=after,
            device_id_type=MESH,
        )

    def gated_copy(c):
        part = pl.ds(c * chunk_cols, chunk_cols)
        return pltpu.make_async_remote_copy(
            gated_s.at[:, part],
            prev_g.at[:, part],
            g_send.at[c],
            g_recv.at[c],
            device_id=after,
            device_id_type=MESH,
        )

    def state_copy(level, slot, offset):
        return pltpu.make_async_remote_copy(
            send_s.at[level],
            recv_s.at[slot],
            s_send.at[slot],
            s_recv.at[slot],
            device_id={"ctx": lax.rem(pos + offset, ctx_count)},
            device_id_type=MESH,
        )

    @pl.when(has_after)
    def _():
        for c in range(early):
            key_copy(c).start()

    @pl.when(jnp.logical_not(has_before))
    def _():
        prev_k[...] = jnp.zeros_like(prev_k)
        prev_g[...] = jnp.zeros_like(prev_g)

    u_place = lax.broadcasted_iota(jnp.int32, (1, GROUP, LANES), 1).astype(jnp.float32)

    def state_tile(j, carry):
        cols = pl.ds(pl.multiple_of(j * LANES, LANES), LANES)
        rate = rate_ref[:, cols]
        shrink = jnp.exp(-rate)
        weight_s[:, cols] = res_ref[:, cols] * jnp.sqrt((1.0 - shrink) * (1.0 + shrink))
        rate3 = rate[:, None, :]
        step = jnp.broadcast_to(jnp.exp(-GROUP * rate)[:, None, :], (modes, GROUP, LANES))
        x = x_ref[:, cols].astype(jnp.float32)
        total = jnp.broadcast_to(x[None, 0:GROUP], (modes, GROUP, LANES))
        for i in range(1, groups):
            total = total * step + x[None, i * GROUP : (i + 1) * GROUP]
        total = total * jnp.exp(-rate3 * (GROUP - 1.0 - u_place))
        state = jnp.sum(total, axis=1)
        state_s[:, cols] = state
        send_s[0, :, cols] = state.astype(jnp.bfloat16)
        return carry

    loads["rate"].wait()
    loads["res"].wait()
    loads["x"].wait()
    lax.fori_loop(0, tiles, state_tile, 0)

    def start_stage(level, base):
        stride, radix = stages[level]
        for m in range(1, radix):

            @pl.when(pos + m * stride < ctx_count)
            def _(m=m):
                state_copy(level, base + m - 1, m * stride).start()

            @pl.when(pos < m * stride)
            def _(m=m):
                recv_s[base + m - 1] = jnp.zeros(recv_s.shape[1:], recv_s.dtype)

    def wait_stage(level, base):
        stride, radix = stages[level]
        for m in range(1, radix):

            @pl.when(pos >= m * stride)
            def _(m=m):
                state_copy(level, base + m - 1, m * stride).wait_recv()

    def spread(cols, start):
        rate = rate_ref[:, cols]
        step = jnp.broadcast_to(jnp.exp(-GROUP * rate)[:, None, :], (modes, GROUP, LANES))
        term = start[:, None, :] * jnp.exp(-rate[:, None, :] * u_place)
        parts = []
        for i in range(groups):
            parts.append(jnp.sum(term, axis=0))
            if i + 1 < groups:
                term = term * step
        return jnp.concatenate(parts, axis=0)

    start_stage(0, 0)

    def taps_tile(j, carry):
        cols = pl.ds(pl.multiple_of(j * LANES, LANES), LANES)
        high, low = split_bf16(spread(cols, weight_s[:, cols]))
        taps_s[0:rows, cols] = high
        taps_s[rows : 2 * rows, cols] = low
        return carry

    lax.fori_loop(0, tiles, taps_tile, 0)

    wide = 2 * LANES

    def transform_part(j):
        cols = pl.ds(pl.multiple_of(j * wide, wide), wide)
        x = x_ref[:, cols]
        taps_high = taps_s[0:rows, cols]
        taps_low = taps_s[rows : 2 * rows, cols]
        spec = jnp.dot(
            fx_s[...], jnp.concatenate([x, x], axis=0), preferred_element_type=jnp.float32
        )
        filt = jnp.dot(
            fk_s[...],
            jnp.concatenate([taps_high, taps_low, taps_high], axis=0),
            preferred_element_type=jnp.float32,
        )
        s_re, s_im = spec[:rows], spec[rows:]
        f_re, f_im = filt[:rows], filt[rows:]
        product = jnp.concatenate([s_re * f_re - s_im * f_im, s_re * f_im + s_im * f_re], axis=0)
        high, low = split_bf16(product)
        return cols, jnp.dot(
            inv_s[...],
            jnp.concatenate([high, low, high], axis=0),
            preferred_element_type=jnp.float32,
        )


    def transform_tile(j, carry):
        for cols, value in [transform_part(2 * j), transform_part(2 * j + 1)]:
            intra_s[:, cols] = value
        return carry

    base = 0
    for level, (stride, radix) in enumerate(stages):
        wait_stage(level, base)
        last = level + 1 == len(stages)

        def combine_tile(j, carry, level=level, stride=stride, radix=radix, base=base, last=last):
            cols = pl.ds(pl.multiple_of(j * LANES, LANES), LANES)
            rate = rate_ref[:, cols] * float(rows)
            entered = jnp.zeros((modes, LANES), jnp.float32)
            total = state_s[:, cols]
            for m in range(1, radix):
                got = recv_s[base + m - 1, :, cols].astype(jnp.float32)
                entered = entered + jnp.exp(-rate * (m * stride - 1.0)) * got
                if not last:
                    total = total + jnp.exp(-rate * (1.0 * m * stride)) * got
            if level > 0:
                entered = entered + enter_s[:, cols]
            enter_s[:, cols] = entered
            if not last:
                state_s[:, cols] = total
                send_s[level + 1, :, cols] = total.astype(jnp.bfloat16)
            return carry

        lax.fori_loop(0, tiles, combine_tile, 0)
        base += radix - 1
        if not last:
            start_stage(level + 1, base)
        if level == 0:

            @pl.when(has_after)
            def _():
                for c in range(early, chunks):
                    key_copy(c).start()

            loads["fwd"].wait()
            loads["inv"].wait()
            high, low = split_bf16(fwd_ref[...])
            fx_s[...] = jnp.concatenate([high, low], axis=1)
            fk_s[...] = jnp.concatenate([high, high, low], axis=1)
            high, low = split_bf16(inv_ref[...])
            inv_s[...] = jnp.concatenate([high, high, low], axis=1)
            lax.fori_loop(0, chans // (2 * wide), transform_tile, 0)
            loads["skip"].wait()
            loads["v"].wait()

    def gated_tile(j, carry):
        cols = pl.ds(pl.multiple_of(j * LANES, LANES), LANES)
        start = weight_s[:, cols] * enter_s[:, cols] * jnp.exp(-rate_ref[:, cols])
        x = x_ref[:, cols].astype(jnp.float32)
        conv = intra_s[:, cols] + spread(cols, start) + skip_ref[:, cols] * x
        conv = conv.astype(jnp.bfloat16)
        conv_ref[:, cols] = conv
        gated = v_ref[:, cols].astype(jnp.float32) * conv.astype(jnp.float32)
        gated_s[:, cols] = gated.astype(jnp.bfloat16)
        return carry

    for c in range(chunks):
        lax.fori_loop(c * HEADS_PER_CHUNK, (c + 1) * HEADS_PER_CHUNK, gated_tile, 0)

        @pl.when(has_after)
        def _(c=c):
            gated_copy(c).start()

    loads["q"].wait()
    loads["k"].wait()
    loads["gain"].wait()

    @pl.when(has_before)
    def _():
        for c in range(chunks):
            key_copy(c).wait_recv()

    q_place = lax.broadcasted_iota(jnp.int32, (rows, rows), 0)
    k_place = lax.broadcasted_iota(jnp.int32, (rows, rows), 1)
    causal = k_place <= q_place
    before_bias = jnp.where(has_before, 0.0, -jnp.inf)
    contract = (((1,), (1,)), ((), ()))

    def weight_chunk(c, carry):
        start = c * chunk_cols
        parts = [
            pl.ds(start + h * HD if isinstance(start, int) else pl.multiple_of(start + h * HD, HD), HD)
            for h in range(HEADS_PER_CHUNK)
        ]
        scale = HD ** (-0.5)
        scores = []
        for cols in parts:
            q = q_ref[:, cols]
            old = lax.dot_general(q, prev_k[:, cols], contract, preferred_element_type=jnp.float32)
            new = lax.dot_general(q, k_ref[:, cols], contract, preferred_element_type=jnp.float32)
            scores.append((old * scale + before_bias, jnp.where(causal, new * scale, -jnp.inf)))
        tops = [jnp.max(jnp.maximum(old, new), axis=1, keepdims=True) for old, new in scores]
        weights = [
            (jnp.exp(old - top), jnp.exp(new - top)) for (old, new), top in zip(scores, tops)
        ]
        totals = [jnp.sum(old + new, axis=1, keepdims=True) for old, new in weights]
        mixes = [
            jnp.dot(new.astype(jnp.bfloat16), gated_s[:, cols], preferred_element_type=jnp.float32)
            for (_, new), cols in zip(weights, parts)
        ]
        for cols, (old, _), total, mix in zip(parts, weights, totals, mixes):
            soft_s[:, cols] = old.astype(jnp.bfloat16)
            own_s[:, cols] = mix
            norm_s[:, cols] = jnp.broadcast_to(1.0 / total, (rows, HD))
        return carry

    lax.fori_loop(0, chunks, weight_chunk, 0)

    energy_s[...] = jnp.zeros_like(energy_s)

    def mix_chunk(c, carry):
        start = c * chunk_cols
        parts = [
            pl.ds(start + h * HD if isinstance(start, int) else pl.multiple_of(start + h * HD, HD), HD)
            for h in range(HEADS_PER_CHUNK)
        ]
        mixes = [
            own_s[:, cols]
            + jnp.dot(soft_s[:, cols], prev_g[:, cols], preferred_element_type=jnp.float32)
            for cols in parts
        ]
        mixes = [(m * norm_s[:, cols]).astype(jnp.bfloat16) for m, cols in zip(mixes, parts)]
        total = energy_s[...]
        for cols, attention in zip(parts, mixes):
            att_s[:, cols] = attention
            attention = attention.astype(jnp.float32)
            total = total + attention * attention
        energy_s[...] = total
        return carry

    for c in range(chunks):

        @pl.when(has_before)
        def _(c=c):
            gated_copy(c).wait_recv()

        mix_chunk(c, 0)

    def energy_copy(o):
        return pltpu.make_async_remote_copy(
            energy_s,
            energy_r.at[o - 1],
            e_send.at[o - 1],
            e_recv.at[o - 1],
            device_id={"ch": lax.rem(core + o, ch_count)},
            device_id_type=MESH,
        )

    for o in range(1, ch_count):
        energy_copy(o).start()
    energy = energy_s[...]
    for o in range(1, ch_count):
        energy_copy(o).wait_recv()
        energy = energy + energy_r[o - 1]
    mean_square = jnp.sum(energy, axis=1, keepdims=True) / float(chans * ch_count)
    factor = jnp.broadcast_to(lax.rsqrt(mean_square + 1e-6), (rows, LANES))

    def norm_tile(j, carry):
        cols = pl.ds(pl.multiple_of(j * LANES, LANES), LANES)
        attention = att_s[:, cols].astype(jnp.float32)
        out_ref[:, cols] = (attention * gain_ref[:, cols] * factor).astype(jnp.bfloat16)
        return carry

    lax.fori_loop(0, tiles, norm_tile, 0)

    for o in range(1, ch_count):
        energy_copy(o).wait_send()

    @pl.when(has_after)
    def _():
        for c in range(chunks):
            key_copy(c).wait_send()
            gated_copy(c).wait_send()

    base = 0
    for level, (stride, radix) in enumerate(stages):
        for m in range(1, radix):

            @pl.when(pos + m * stride < ctx_count)
            def _(level=level, slot=base + m - 1, offset=m * stride):
                state_copy(level, slot, offset).wait_send()

        base += radix - 1


def per_device(
    conv_input, residues, decay_rates, skip_gain, query_rows, key_rows, value_rows, norm_gain
):
    ctx_count = lax.axis_size("ctx")
    ch_count = lax.axis_size("ch")
    rows, chans = conv_input.shape
    modes = residues.shape[1]
    chunks = chans // (HEADS_PER_CHUNK * HD)
    stages = scan_stages(ctx_count)
    slots = sum(radix - 1 for _, radix in stages)
    fwd, inv = (jnp.asarray(t) for t in dft_tables(rows))
    flat = jax.ShapeDtypeStruct((rows, chans), jnp.bfloat16)
    vmem = pl.BlockSpec(memory_space=pltpu.VMEM)
    hbm = pl.BlockSpec(memory_space=pltpu.HBM)
    dma = pltpu.SemaphoreType.DMA
    f32, b16 = jnp.float32, jnp.bfloat16
    return pl.pallas_call(
        functools.partial(kernel, ctx_count, ch_count),
        out_shape=(flat, flat),
        in_specs=[hbm] * 10,
        out_specs=(vmem, vmem),
        scratch_shapes=[
            pltpu.VMEM((rows, chans), b16),
            pltpu.VMEM((modes, chans), f32),
            pltpu.VMEM((modes, chans), f32),
            pltpu.VMEM((1, chans), f32),
            pltpu.VMEM((rows, chans), b16),
            pltpu.VMEM((rows, chans), b16),
            pltpu.VMEM((rows, chans), b16),
            pltpu.VMEM((1, chans), f32),
            pltpu.VMEM(fwd.shape, f32),
            pltpu.VMEM(inv.shape, f32),
            pltpu.VMEM((2 * rows, 2 * rows), b16),
            pltpu.VMEM((2 * rows, 3 * rows), b16),
            pltpu.VMEM((rows, 6 * rows), b16),
            dma((10,)),
            pltpu.VMEM((modes, chans), f32),
            pltpu.VMEM((2 * rows, chans), b16),
            pltpu.VMEM((rows, chans), f32),
            pltpu.VMEM((modes, chans), f32),
            pltpu.VMEM((modes, chans), f32),
            pltpu.VMEM((len(stages), modes, chans), b16),
            pltpu.VMEM((slots, modes, chans), b16),
            pltpu.VMEM((rows, chans), b16),
            pltpu.VMEM((rows, chans), b16),
            pltpu.VMEM((rows, chans), b16),
            pltpu.VMEM((rows, chans), b16),
            pltpu.VMEM((rows, chans), f32),
            pltpu.VMEM((rows, chans), f32),
            pltpu.VMEM((rows, chans), b16),
            pltpu.VMEM((rows, LANES), f32),
            pltpu.VMEM((ch_count - 1, rows, LANES), f32),
            dma((chunks,)),
            dma((chunks,)),
            dma((chunks,)),
            dma((chunks,)),
            dma((slots,)),
            dma((slots,)),
            dma((ch_count - 1,)),
            dma((ch_count - 1,)),
        ],
        compiler_params=pltpu.CompilerParams(
            collective_id=0, has_side_effects=True, vmem_limit_bytes=63 * 1024 * 1024
        ),
        cost_estimate=pl.CostEstimate(
            flops=4 * 10**9, bytes_accessed=4 * 10**6, transcendentals=10**6
        ),
    )(
        conv_input,
        jnp.transpose(decay_rates),
        jnp.transpose(residues),
        skip_gain[None, :],
        query_rows,
        key_rows,
        value_rows,
        norm_gain[None, :],
        fwd,
        inv,
    )


def solution(mesh):
    return jax.shard_map(
        per_device,
        mesh=mesh,
        in_specs=(
            P("ctx", "ch"),
            P("ch", None),
            P("ch", None),
            P("ch"),
            P("ctx", "ch"),
            P("ctx", "ch"),
            P("ctx", "ch"),
            P("ch"),
        ),
        out_specs=(P("ctx", "ch"), P("ctx", "ch")),
        check_vma=False,
    )
```
